512 devices in a mesh: stream: 32 (over x, y_hi, core), cross: 16 (over z, y_lo).
Axes of the slice: x: 4, y: 8 (y_hi: 4, y_lo: 2; y = y_hi * 2 + y_lo), z: 8, core: 2. Of those that a mesh axis runs over, the one named last changes fastest.
Arguments:
- latents: bfloat16 [262144, 128], P(('stream', 'cross')), may hold values from -6 to 6
- stale_latents: bfloat16 [262144, 128], P(('stream', 'cross')), may hold values from -6 to 6
- edge_latents: bfloat16 [786432, 128], P(('stream', 'cross')), may hold values from -6 to 6
- senders: int32 [786432], P(('stream', 'cross')), may hold values from 0 to 1023
- receivers: int32 [786432], P(('stream', 'cross')), may hold values from 0 to 511
- edge_count: int32 [512], P(('stream', 'cross')), may hold values from 512 to 1536, as said below
- send_list: int32 [512, 4, 128], P(('stream', 'cross')), may hold values from 0 to 511
- node_cotangent: bfloat16 [262144, 128], P(('stream', 'cross')), may hold values from -6 to 6
- edge_cotangent: bfloat16 [786432, 128], P(('stream', 'cross')), may hold values from -6 to 6
- edge_first: bfloat16 [384, 128], replicated, may hold values from -0.3125 to 0.3125
- edge_bias: float32 [128], replicated, may hold values from -3 to 3
- edge_second: bfloat16 [128, 128], replicated, may hold values from -0.5 to 0.5
- edge_gain: float32 [128], replicated, may hold values from 0.25 to 1.75
- node_first: bfloat16 [256, 128], replicated, may hold values from -0.375 to 0.375
- node_bias: float32 [128], replicated, may hold values from -3 to 3
- node_second: bfloat16 [128, 128], replicated, may hold values from -0.5 to 0.5
- node_gain: float32 [128], replicated, may hold values from 0.25 to 1.75
Outputs:
- new_latents: bfloat16 [262144, 128], P(('stream', 'cross'))
- latent_grads: bfloat16 [262144, 128], P(('stream', 'cross'))
- stale_grads: bfloat16 [262144, 128], P(('stream', 'cross'))
- edge_grads: bfloat16 [786432, 128], P(('stream', 'cross'))
- edge_first_grad: float32 [384, 128], replicated
- edge_bias_grad: float32 [128], replicated
- edge_second_grad: float32 [128, 128], replicated
- edge_gain_grad: float32 [128], replicated
- node_first_grad: float32 [256, 128], replicated
- node_bias_grad: float32 [128], replicated
- node_second_grad: float32 [128, 128], replicated
- node_gain_grad: float32 [128], replicated
The draws below stay inside these ranges and needn't reach their ends.
Inputs may be any that keep to these rules, and one draw needn't show every extreme that they name: `edge_count`: a partition's live edge slots come first; some partition has 1536 live slots. `senders`: rows below 512 are the partition's own nodes, the rest its four halo blocks in the order of the steps. `send_list`: a row may be listed more than once.
All inputs are finite; a program needn't handle non-finite values.
Results may differ from the reference program's by a relative error of at most 0.015.
Values may be sent and summed in bfloat16 or wider, within the bound.
A program may use at most 64 MiB of HBM per device.

```python
import math
import jax
import jax.numpy as jnp
from jax import lax

WIDTH = 128
NODES_DEV = 512
HALO = 128
EDGES_DEV = 1536
NODES = 262144
EDGES = 786432
N_STREAM = 32
N_CROSS = 16
DEVICES = 512


def draw_edge_count(key, part):
    first_key, second_key = jax.random.split(jax.random.fold_in(key, 11))
    counts = jax.random.randint(first_key, (DEVICES,), EDGES_DEV // 3, EDGES_DEV + 1)
    chosen = jax.random.randint(second_key, (), 0, DEVICES)
    return jnp.where(jnp.arange(DEVICES) == chosen, EDGES_DEV, counts).astype(jnp.int32)


def set_ends(values, key, smallest, top_value):
    spot = [jax.random.randint(jax.random.fold_in(key, axis), (), 0, length) for axis, length in enumerate(values.shape)]
    longest = values.shape.index(max(values.shape))
    neighbour = spot[:longest] + [(spot[longest] + 1) % values.shape[longest]] + spot[longest + 1:]
    return values.at[tuple(spot)].set(smallest).at[tuple(neighbour)].set(top_value)


def level_of(stream_key, shape, pieces, smallest, top_value):
    factor_of = 1.0
    for position, shards_of in pieces:
        draws = jax.random.uniform(jax.random.fold_in(jax.random.fold_in(stream_key, 6), position), (shards_of,), jnp.float32, smallest / len(pieces), top_value / len(pieces))
        factor_of = factor_of * jnp.repeat(jnp.exp(draws), shape[position] // shards_of).reshape((-1,) + (1,) * (len(shape) - 1 - position))
    return factor_of


def noise(rng, dims, spread, most, pieces=(), held_as=jnp.bfloat16):
    result = spread * jax.random.normal(rng, dims, jnp.float32)
    if pieces:
        result = result * level_of(rng, dims, pieces, -0.22, 0.18)
    return jnp.clip(result, -most, most).astype(held_as)


def setup_inputs(seed: int = 0) -> dict:
    keys = jax.random.split(jax.random.key(seed), 18)
    latents = noise(keys[0], (NODES, WIDTH), 1.0, 6.0, ((0, 512),))
    stale_latents = noise(keys[1], (NODES, WIDTH), 1.0, 6.0, ((0, 512),))
    edge_latents = noise(keys[2], (EDGES, WIDTH), 1.0, 6.0, ((0, 512),))
    senders = set_ends(jax.random.randint(keys[3], (EDGES,), 0, NODES_DEV + 4 * HALO), jax.random.fold_in(keys[3], 1), 0, (NODES_DEV + 4 * HALO) - 1).astype(jnp.int32)
    receivers = set_ends(jax.random.randint(keys[4], (EDGES,), 0, NODES_DEV), jax.random.fold_in(keys[4], 1), 0, NODES_DEV - 1).astype(jnp.int32)
    edge_count = draw_edge_count(jax.random.fold_in(keys[17], 71), 0)
    send_list = set_ends(jax.random.randint(keys[6], (DEVICES, 4, HALO), 0, NODES_DEV), jax.random.fold_in(keys[6], 1), 0, NODES_DEV - 1).astype(jnp.int32)
    node_cotangent = noise(keys[7], (NODES, WIDTH), 1.0, 6.0, ((0, 512),))
    edge_cotangent = noise(keys[8], (EDGES, WIDTH), 1.0, 6.0, ((0, 512),))
    edge_first = noise(keys[9], (3 * WIDTH, WIDTH), (3 * WIDTH) ** -0.5, 0.3125)
    edge_bias = noise(keys[10], (WIDTH,), 0.5, 3.0, (), jnp.float32)
    edge_second = noise(keys[11], (WIDTH, WIDTH), WIDTH ** -0.5, 0.5)
    edge_gain = jnp.clip(1.0 + 0.15 * jax.random.normal(keys[12], (WIDTH,), jnp.float32), 0.25, 1.75)
    node_first = noise(keys[13], (2 * WIDTH, WIDTH), (2 * WIDTH) ** -0.5, 0.375)
    node_bias = noise(keys[14], (WIDTH,), 0.5, 3.0, (), jnp.float32)
    node_second = noise(keys[15], (WIDTH, WIDTH), WIDTH ** -0.5, 0.5)
    node_gain = jnp.clip(1.0 + 0.15 * jax.random.normal(keys[16], (WIDTH,), jnp.float32), 0.25, 1.75)
    return {"latents": latents, "stale_latents": stale_latents, "edge_latents": edge_latents, "senders": senders, "receivers": receivers, "edge_count": edge_count, "send_list": send_list, "node_cotangent": node_cotangent, "edge_cotangent": edge_cotangent, "edge_first": edge_first, "edge_bias": edge_bias, "edge_second": edge_second, "edge_gain": edge_gain, "node_first": node_first, "node_bias": node_bias, "node_second": node_second, "node_gain": node_gain}


EPSILON = 1e-05

def layer_norm(values, scale_gain):
    row_mean = lax.optimization_barrier(jnp.mean(values, axis=-1, keepdims=True))
    centered = values - row_mean
    variance = lax.optimization_barrier(jnp.mean(centered * centered, axis=-1, keepdims=True))
    return centered * lax.rsqrt(variance + EPSILON) * scale_gain

def local_layer(owned, halo_rows, edge_rows, params, senders, receivers, edge_total):
    edge_first, edge_bias, edge_second, edge_gain, node_first, node_bias, node_second, node_gain = params
    node_table = jnp.concatenate([owned, halo_rows], axis=0)
    sender_rows = jnp.take(node_table, senders, axis=0)
    receiver_rows = jnp.take(owned, receivers, axis=0)
    joined = jnp.concatenate([edge_rows, sender_rows, receiver_rows], axis=1).astype(jnp.bfloat16)
    hidden_pre = jnp.dot(joined, edge_first, preferred_element_type=jnp.float32) + edge_bias
    edge_hidden = jax.nn.silu(hidden_pre).astype(jnp.bfloat16)
    edge_out = jnp.dot(edge_hidden, edge_second, preferred_element_type=jnp.float32)
    edge_alive = (jnp.arange(edge_rows.shape[0], dtype=jnp.int32) < edge_total).astype(jnp.float32)[:, None]
    new_edges = (edge_rows + edge_alive * layer_norm(edge_out, edge_gain)).astype(jnp.bfloat16)
    summed = jnp.zeros(owned.shape, jnp.float32).at[receivers].add(edge_alive * new_edges.astype(jnp.float32))
    node_input = jnp.concatenate([owned, summed], axis=1).astype(jnp.bfloat16)
    node_pre = jnp.dot(node_input, node_first, preferred_element_type=jnp.float32) + node_bias
    node_hidden = jax.nn.silu(node_pre).astype(jnp.bfloat16)
    node_out = jnp.dot(node_hidden, node_second, preferred_element_type=jnp.float32)
    new_latents = (owned + layer_norm(node_out, node_gain)).astype(jnp.bfloat16)
    return (new_latents, new_edges)

def local_step(latent_block, halo_block, edge_block, params, senders, receivers, edge_total, node_cot, edge_cot):

    def forward(owned, halo_rows, edge_rows, weights):
        return local_layer(owned, halo_rows, edge_rows, weights, senders, receivers, edge_total)
    outputs, pullback = jax.vjp(forward, latent_block.astype(jnp.float32), halo_block.astype(jnp.float32), edge_block.astype(jnp.float32), params)
    grad_owned, grad_halo, grad_edges, grad_params = pullback((node_cot.astype(outputs[0].dtype), edge_cot.astype(outputs[1].dtype)))
    grad_params = tuple((item.astype(jnp.float32) for item in grad_params))
    return (outputs[0], grad_owned, grad_halo, grad_edges, grad_params)

def reference(latents, stale_latents, edge_latents, senders, receivers, edge_count, send_list, node_cotangent, edge_cotangent, edge_first, edge_bias, edge_second, edge_gain, node_first, node_bias, node_second, node_gain):
    rows_s = N_STREAM
    rows_c = N_CROSS
    width = latents.shape[1]
    parts = rows_s * rows_c
    owned_all = latents.reshape(parts, NODES_DEV, width)
    stale_all = stale_latents.reshape(parts, NODES_DEV, width)
    send_rows = send_list.reshape(parts, 4 * HALO)
    picked = jax.vmap(lambda table, index: jnp.take(table, index, axis=0))(stale_all, send_rows)
    picked = picked.reshape(rows_s, rows_c, 4, HALO, width)
    zeros_s = jnp.zeros((1, rows_c, HALO, width), picked.dtype)
    zeros_c = jnp.zeros((rows_s, 1, HALO, width), picked.dtype)
    block_zero = jnp.concatenate([zeros_s, picked[:-1, :, 0]], axis=0)
    block_one = jnp.concatenate([picked[1:, :, 1], zeros_s], axis=0)
    block_two = jnp.concatenate([zeros_c, picked[:, :-1, 2]], axis=1)
    block_three = jnp.concatenate([picked[:, 1:, 3], zeros_c], axis=1)
    halo_all = jnp.stack([block_zero, block_one, block_two, block_three], axis=2).reshape(parts, 4 * HALO, width)
    params = (edge_first, edge_bias, edge_second, edge_gain, node_first, node_bias, node_second, node_gain)

    def one_part(items):
        owned, halo_rows, edge_rows, send_idx, recv_idx, edge_total, node_cot, edge_cot = items
        return local_step(owned, halo_rows, edge_rows, params, send_idx, recv_idx, edge_total, node_cot, edge_cot)
    items = (owned_all, halo_all, edge_latents.reshape(parts, EDGES_DEV, width), senders.reshape(parts, EDGES_DEV), receivers.reshape(parts, EDGES_DEV), edge_count, node_cotangent.reshape(parts, NODES_DEV, width), edge_cotangent.reshape(parts, EDGES_DEV, width))
    new_latents, grad_owned, grad_halo, grad_edges, grad_params = lax.map(one_part, items)
    halo_grads = grad_halo.reshape(rows_s, rows_c, 4, HALO, width)
    fzero_s = jnp.zeros((1, rows_c, HALO, width), jnp.float32)
    fzero_c = jnp.zeros((rows_s, 1, HALO, width), jnp.float32)
    back_zero = jnp.concatenate([halo_grads[1:, :, 0], fzero_s], axis=0)
    back_one = jnp.concatenate([fzero_s, halo_grads[:-1, :, 1]], axis=0)
    back_two = jnp.concatenate([halo_grads[:, 1:, 2], fzero_c], axis=1)
    back_three = jnp.concatenate([fzero_c, halo_grads[:, :-1, 3]], axis=1)
    returned = jnp.stack([back_zero, back_one, back_two, back_three], axis=2).reshape(parts, 4 * HALO, width)
    stale_grads = jax.vmap(lambda index, values: jnp.zeros((NODES_DEV, width), jnp.float32).at[index].add(values))(send_rows, returned)
    totals = tuple((lax.optimization_barrier(jnp.sum(item, axis=0)) for item in grad_params))
    squares = jnp.zeros((), jnp.float32)
    entries = 0
    for item in totals:
        squares = squares + jnp.sum(item * item)
        entries = entries + item.size
    factor = jnp.minimum(1.0, math.sqrt(entries) * lax.rsqrt(squares))
    clipped = tuple((item * factor for item in totals))
    return (new_latents.reshape(parts * NODES_DEV, width), grad_owned.astype(jnp.bfloat16).reshape(parts * NODES_DEV, width), stale_grads.astype(jnp.bfloat16).reshape(parts * NODES_DEV, width), grad_edges.astype(jnp.bfloat16).reshape(parts * EDGES_DEV, width), clipped[0], clipped[1], clipped[2], clipped[3], clipped[4], clipped[5], clipped[6], clipped[7])
```

```python
import math

import jax
import jax.numpy as jnp
from jax import lax
from jax.experimental import pallas as pl
from jax.experimental.pallas import tpu as pltpu
from jax.sharding import PartitionSpec as P

EPSILON = 1e-05
MESH = pl.DeviceIdType.MESH
F32 = jnp.float32
BF16 = jnp.bfloat16
W = 128
NODES = 512
EDGES = 1536
HALO = 128
CHUNK = 256
TILE = 32
NEAR = 32
FAR = 16
PACK = TILE * NEAR
ROW_NODE_FIRST = 0
ROW_NODE_SECOND = 256
ROW_EDGE_SECOND = 384
ROW_EDGE_FIRST = 512
ROW_SMALL = 896

CORE = ("s", 1, 2)
Y_HI = ("s", 2, 4)
X = ("s", 8, 4)
Y_LO = ("c", 1, 2)
Z_0 = ("c", 2, 2)
Z_HI = ("c", 4, 4)


class Group:
    def __init__(self, digits, s, c):
        self.s, self.c = s, c
        self.pos = 0
        self.peers = [(0, 0, 0, 0)]
        size = 1
        for axis, stride, n in digits:
            d = ((s if axis == "s" else c) // stride) % n
            self.pos = self.pos + d * size
            grown = []
            for k in range(n):
                q = (d + k) % n if k else d
                step = (q - d) * stride if k else 0
                for key, ds, dc, at in self.peers:
                    grown.append(
                        (
                            key + k * size,
                            ds + step if axis == "s" else ds,
                            dc + step if axis == "c" else dc,
                            at + q * size,
                        )
                    )
            self.peers = grown
            size *= n
        self.size = size
        self.peers = sorted(self.peers, key=lambda p: p[0])[1:]

    def others(self):
        for key, ds, dc, at in self.peers:
            yield key, (self.s + ds, self.c + dc), at


def dot(a, b):
    return jnp.dot(a, b, preferred_element_type=F32)


def dot_nt(a, b):
    return lax.dot_general(a, b, (((1,), (1,)), ((), ())), preferred_element_type=F32)


def dot_tn(a, b):
    return lax.dot_general(a, b, (((0,), (0,)), ((), ())), preferred_element_type=F32)


def columns_of(ref, first, count):
    parts = []
    for k in range(count):
        row = ref[pl.ds(first + k, 1), :]
        parts.append(jnp.broadcast_to(row, (W, W)).T)
    return parts[0] if count == 1 else jnp.concatenate(parts, axis=0)


def hot_rows(col, blocks):
    lane = lax.broadcasted_iota(jnp.int32, col.shape, 1)
    return jnp.concatenate(
        [jnp.where(col == lane + W * j, 1.0, 0.0).astype(BF16) for j in range(blocks)], axis=1
    )


def hot_cols(row, height):
    at = lax.broadcasted_iota(jnp.int32, (height, row.shape[1]), 0)
    return jnp.where(at == row, 1.0, 0.0).astype(BF16)


def sigmoid(v):
    return 0.5 * jnp.tanh(0.5 * v) + 0.5


def normed(z):
    centered = z - jnp.mean(z, axis=-1, keepdims=True)
    rstd = lax.rsqrt(jnp.mean(centered * centered, axis=-1, keepdims=True) + EPSILON)
    return centered * rstd, rstd


def normed_back(dx, xhat, rstd):
    m1 = jnp.mean(dx, axis=-1, keepdims=True)
    m2 = jnp.mean(dx * xhat, axis=-1, keepdims=True)
    return rstd * (dx - m1 - xhat * m2)


def place():
    s = lax.axis_index("stream")
    c = lax.axis_index("cross")
    ns = lax.axis_size("stream")
    nc = lax.axis_size("cross")
    to = [((s + 1, c), s < ns - 1), ((s - 1, c), s > 0), ((s, c + 1), c < nc - 1), ((s, c - 1), c > 0)]
    count = sum(ok.astype(jnp.int32) for _, ok in to)
    return s, c, to, count


BACK = (1, 0, 3, 2)


def halo_kernel(stale_ref, list_ref, halo_ref, picked, landed, send_sem, recv_sem):
    s, c, to, count = place()
    barrier = pltpu.get_barrier_semaphore()
    for where, ok in to:

        @pl.when(ok)
        def _(where=where):
            pl.semaphore_signal(barrier, inc=1, device_id=where, device_id_type=MESH)

    table = jnp.concatenate([stale_ref[:256, :], stale_ref[256:, :]], axis=1)
    for k in range(4):
        col = columns_of(list_ref, k, 1)
        both = dot(hot_rows(col & 255, 2), table)
        picked[k] = jnp.where(col < 256, both[:, :W], both[:, W:]).astype(BF16)

    pl.semaphore_wait(barrier, count)

    def copy(k):
        return pltpu.make_async_remote_copy(
            src_ref=picked.at[k],
            dst_ref=landed.at[k],
            send_sem=send_sem.at[k],
            recv_sem=recv_sem.at[k],
            device_id=to[k][0],
            device_id_type=MESH,
        )

    for k in range(4):

        @pl.when(to[k][1])
        def _(k=k):
            copy(k).start()

    for k in range(4):
        has = to[BACK[k]][1]

        @pl.when(has)
        def _(k=k):
            copy(k).wait_recv()
            halo_ref[HALO * k : HALO * (k + 1), :] = landed[k]

        @pl.when(jnp.logical_not(has))
        def _(k=k):
            halo_ref[HALO * k : HALO * (k + 1), :] = jnp.zeros((HALO, W), BF16)

    for k in range(4):

        @pl.when(to[k][1])
        def _(k=k):
            copy(k).wait_send()


def layer_kernel(
    lat_ref,
    halo_ref,
    edge_ref,
    snd_ref,
    rcv_ref,
    count_ref,
    list_ref,
    ncot_ref,
    ecot_ref,
    w1_ref,
    b1_ref,
    w2_ref,
    g_ref,
    nw1_ref,
    nb1_ref,
    nw2_ref,
    ng_ref,
    new_ref,
    latg_ref,
    staleg_ref,
    edgeg_ref,
    gw1_ref,
    gb1_ref,
    gw2_ref,
    gg_ref,
    gnw1_ref,
    gnb1_ref,
    gnw2_ref,
    gng_ref,
    hot_r,
    rows_sr,
    hidden,
    slope,
    xhat_s,
    rstd_s,
    values,
    d_pre,
    pack,
    near_in,
    near_sum,
    far_in,
    far_sum,
    total,
    halo_out,
    halo_in,
    near_send,
    near_recv,
    far_send,
    far_recv,
    all_send,
    all_recv,
    halo_send,
    halo_recv,
):
    s, c, to, count = place()
    near = Group((CORE, X, Y_LO, Z_0), s, c)
    far = Group((Y_HI, Z_HI), s, c)
    barrier = pltpu.get_barrier_semaphore()
    for where, ok in to:

        @pl.when(ok)
        def _(where=where):
            pl.semaphore_signal(barrier, inc=1, device_id=where, device_id_type=MESH)

    for group in (far, near):
        for _, where, _ in group.others():
            pl.semaphore_signal(barrier, inc=1, device_id=where, device_id_type=MESH)

    alive_count = count_ref[0]
    lat = lat_ref[...]
    table_s = jnp.concatenate([lat, halo_ref[...]], axis=1)
    table_r = jnp.concatenate([lat[:256, :], lat[256:, :]], axis=1)
    gain = g_ref[...]
    per = CHUNK // W

    def alive_rows(i):
        at = lax.broadcasted_iota(jnp.int32, (CHUNK, W), 0) + i * CHUNK
        return at < alive_count

    def forward(i, carry):
        at = pl.ds(pl.multiple_of(i * CHUNK, CHUNK), CHUNK)
        col_s = columns_of(snd_ref, i * per, per)
        col_r = columns_of(rcv_ref, i * per, per)
        alive = alive_rows(i)
        both = dot(hot_rows(col_s & 511, 4), table_s)
        rows_s = jnp.where(col_s < 512, both[:, :W], both[:, W:]).astype(BF16)
        hot = hot_rows(jnp.where(alive, col_r & 255, -1), 2)
        hot_r[at, :] = hot
        both = dot(hot, table_r)
        low = col_r < 256
        rows_r = jnp.where(low, both[:, :W], both[:, W:]).astype(BF16)
        edge = edge_ref[at, :]
        joined = jnp.concatenate([edge, rows_s, rows_r], axis=1)
        rows_sr[at, :] = joined
        pre = dot(joined, w1_ref[...]) + b1_ref[...]
        gate = sigmoid(pre)
        act = pre * gate
        slope[at, :] = gate + act * (1.0 - gate)
        act = act.astype(BF16)
        hidden[at, :] = act
        xhat, rstd = normed(dot(act, w2_ref[...]))
        xhat_s[at, :] = xhat
        rstd_s[at, :] = jnp.broadcast_to(rstd, xhat.shape)
        new = edge.astype(F32) + xhat * gain
        values[at, :] = jnp.concatenate(
            [jnp.where(low, new, 0.0).astype(BF16), jnp.where(low, 0.0, new).astype(BF16)], axis=1
        )
        return carry

    lax.fori_loop(0, EDGES // CHUNK, forward, 0)

    def masked_receivers():
        at = lax.broadcasted_iota(jnp.int32, (1, W), 1)
        rows = []
        for k in range(EDGES // W):
            rows.append(jnp.where(at + k * W < alive_count, rcv_ref[k : k + 1, :] & 255, -1))
        return jnp.concatenate(rows, axis=1)

    hot_rt = hot_cols(masked_receivers(), 256)
    agg = dot(hot_rt, values[...])
    agg = jnp.concatenate([agg[:, :W], agg[:, W:]], axis=0).astype(BF16)

    node_in = jnp.concatenate([lat, agg], axis=1)
    pre = dot(node_in, nw1_ref[...]) + nb1_ref[...]
    gate = sigmoid(pre)
    act = pre * gate
    node_slope = gate + act * (1.0 - gate)
    act = act.astype(BF16)
    xhat, rstd = normed(dot(act, nw2_ref[...]))
    ngain = ng_ref[...]
    new_ref[...] = (lat.astype(F32) + xhat * ngain).astype(BF16)
    dy = ncot_ref[...].astype(F32)
    d_ngain = jnp.sum(dy * xhat, axis=0, keepdims=True)
    dz = normed_back(dy * ngain, xhat, rstd).astype(BF16)
    pack[ROW_NODE_SECOND : ROW_NODE_SECOND + 128, :] = dot_tn(act, dz).astype(BF16)
    dp = dot_nt(dz, nw2_ref[...]) * node_slope
    d_nbias = jnp.sum(dp, axis=0, keepdims=True)
    dp = dp.astype(BF16)
    pack[ROW_NODE_FIRST : ROW_NODE_FIRST + 256, :] = dot_tn(node_in, dp).astype(BF16)
    d_in = dot_nt(dp, nw1_ref[...])
    own = dy + d_in[:, :W]
    d_agg = d_in[:, W:].astype(BF16)
    table_d = jnp.concatenate([d_agg[:256, :], d_agg[256:, :]], axis=1)

    def backward(i, carry):
        d_gain, d_bias = carry
        at = pl.ds(pl.multiple_of(i * CHUNK, CHUNK), CHUNK)
        col_r = columns_of(rcv_ref, i * per, per)
        both = dot(hot_r[at, :], table_d)
        ct = ecot_ref[at, :].astype(F32) + jnp.where(col_r < 256, both[:, :W], both[:, W:])
        dy = jnp.where(alive_rows(i), ct, 0.0)
        xhat = xhat_s[at, :]
        d_gain = d_gain + jnp.sum(dy * xhat, axis=0, keepdims=True)
        dz = normed_back(dy * gain, xhat, rstd_s[at, :]).astype(BF16)
        dp = dot_nt(dz, w2_ref[...]) * slope[at, :]
        d_bias = d_bias + jnp.sum(dp, axis=0, keepdims=True)
        d_pre[at, :] = dp.astype(BF16)
        xhat_s[at, :] = ct
        values[at, :W] = dz
        return d_gain, d_bias

    zero = jnp.zeros((1, W), F32)
    d_gain, d_bias = lax.fori_loop(0, EDGES // CHUNK, backward, (zero, zero))
    pack[ROW_EDGE_SECOND : ROW_EDGE_SECOND + 128, :] = dot_tn(hidden[...], values[:, :W]).astype(BF16)
    pack[ROW_EDGE_FIRST : ROW_EDGE_FIRST + 384, :] = dot_tn(rows_sr[...], d_pre[...]).astype(BF16)
    pack[ROW_SMALL:, :] = jnp.concatenate(
        [d_bias, d_gain, d_nbias, d_ngain, jnp.zeros((PACK - ROW_SMALL - 4, W), F32)], axis=0
    ).astype(BF16)

    pl.semaphore_wait(barrier, count + (NEAR - 1) + (FAR - 1))
    for key, where, at in near.others():
        pltpu.make_async_remote_copy(
            src_ref=pack.at[pl.ds(pl.multiple_of(at * TILE, TILE), TILE)],
            dst_ref=near_in.at[key - 1],
            send_sem=near_send,
            recv_sem=near_recv,
            device_id=where,
            device_id_type=MESH,
        ).start()

    def spread(i, carry):
        at = pl.ds(pl.multiple_of(i * CHUNK, CHUNK), CHUNK)
        d_joined = dot_nt(d_pre[at, :], w1_ref[...])
        edgeg_ref[at, :] = (xhat_s[at, :] + d_joined[:, :W]).astype(BF16)
        mine = columns_of(snd_ref, i * per, per) < 512
        d_s = d_joined[:, W : 2 * W]
        values[at, :] = jnp.concatenate(
            [jnp.where(mine, d_s, 0.0).astype(BF16), jnp.where(mine, 0.0, d_s).astype(BF16)], axis=1
        )
        low = columns_of(rcv_ref, i * per, per) < 256
        d_r = d_joined[:, 2 * W :]
        rows_sr[at, : 2 * W] = jnp.concatenate(
            [jnp.where(low, d_r, 0.0).astype(BF16), jnp.where(low, 0.0, d_r).astype(BF16)], axis=1
        )
        return carry

    lax.fori_loop(0, EDGES // CHUNK, spread, 0)
    senders = jnp.concatenate([snd_ref[k : k + 1, :] & 511 for k in range(EDGES // W)], axis=1)
    spread_s = dot(hot_cols(senders, 512), values[...])
    for k in range(4):
        halo_out[k] = spread_s[HALO * k : HALO * (k + 1), W:].astype(BF16)

    def back(k):
        return pltpu.make_async_remote_copy(
            src_ref=halo_out.at[k],
            dst_ref=halo_in.at[k],
            send_sem=halo_send.at[k],
            recv_sem=halo_recv.at[k],
            device_id=to[BACK[k]][0],
            device_id_type=MESH,
        )

    for k in range(4):

        @pl.when(to[BACK[k]][1])
        def _(k=k):
            back(k).start()

    spread_r = dot(hot_cols(masked_receivers(), 256), rows_sr[:, : 2 * W])
    latg_ref[...] = (
        own + spread_s[:, :W] + jnp.concatenate([spread_r[:, :W], spread_r[:, W:]], axis=0)
    ).astype(BF16)

    mine = pl.ds(pl.multiple_of(near.pos * TILE, TILE), TILE)
    pltpu.make_async_copy(near_in, near_in, near_recv).wait()
    acc = pack[mine, :].astype(F32)
    for k in range(NEAR - 1):
        acc = acc + near_in[k].astype(F32)
    near_sum[...] = acc.astype(BF16)
    for key, where, at in far.others():
        pltpu.make_async_remote_copy(
            src_ref=near_sum,
            dst_ref=far_in.at[far.pos],
            send_sem=far_send,
            recv_sem=far_recv,
            device_id=where,
            device_id_type=MESH,
        ).start()

    for k in range(4):
        has = to[k][1]

        @pl.when(has)
        def _(k=k):
            back(k).wait_recv()

        @pl.when(jnp.logical_not(has))
        def _(k=k):
            halo_in[k] = jnp.zeros((HALO, W), BF16)

    parts = []
    for k in range(4):
        low = columns_of(list_ref, k, 1) < 256
        came = halo_in[k].astype(F32)
        parts.append(
            jnp.concatenate(
                [jnp.where(low, came, 0.0).astype(BF16), jnp.where(low, 0.0, came).astype(BF16)],
                axis=1,
            )
        )
    listed = jnp.concatenate([list_ref[k : k + 1, :] & 255 for k in range(4)], axis=1)
    stale = dot(hot_cols(listed, 256), jnp.concatenate(parts, axis=0))
    staleg_ref[...] = jnp.concatenate([stale[:, :W], stale[:, W:]], axis=0).astype(BF16)

    pltpu.make_async_copy(far_in.at[pl.ds(0, FAR - 1)], far_in.at[pl.ds(0, FAR - 1)], far_recv).wait()
    far_in[far.pos] = near_sum[...]
    acc = far_in[0].astype(F32)
    for k in range(1, FAR):
        acc = acc + far_in[k].astype(F32)
    far_sum[...] = acc.astype(BF16)
    for key, where, at in near.others():
        pltpu.make_async_remote_copy(
            src_ref=far_sum,
            dst_ref=total.at[mine],
            send_sem=all_send,
            recv_sem=all_recv,
            device_id=where,
            device_id_type=MESH,
        ).start()
    rest = total.at[pl.ds(0, PACK - TILE)]
    pltpu.make_async_copy(rest, rest, all_recv).wait()
    total[mine, :] = far_sum[...]
    sums = total[...].astype(F32)
    entries = ROW_SMALL * W + 4 * W
    squares = jnp.sum(sums * sums)
    factor = jnp.minimum(1.0, math.sqrt(entries) * lax.rsqrt(jnp.full((1, W), squares, F32)))
    sums = sums * factor
    gnw1_ref[...] = sums[ROW_NODE_FIRST : ROW_NODE_FIRST + 256, :]
    gnw2_ref[...] = sums[ROW_NODE_SECOND : ROW_NODE_SECOND + 128, :]
    gw2_ref[...] = sums[ROW_EDGE_SECOND : ROW_EDGE_SECOND + 128, :]
    gw1_ref[...] = sums[ROW_EDGE_FIRST : ROW_EDGE_FIRST + 384, :]
    gb1_ref[...] = sums[ROW_SMALL : ROW_SMALL + 1, :]
    gg_ref[...] = sums[ROW_SMALL + 1 : ROW_SMALL + 2, :]
    gnb1_ref[...] = sums[ROW_SMALL + 2 : ROW_SMALL + 3, :]
    gng_ref[...] = sums[ROW_SMALL + 3 : ROW_SMALL + 4, :]

    for k in range(4):

        @pl.when(to[BACK[k]][1])
        def _(k=k):
            back(k).wait_send()

    pltpu.make_async_copy(near_in, near_in, near_send).wait()
    pltpu.make_async_copy(far_in.at[pl.ds(0, FAR - 1)], far_in.at[pl.ds(0, FAR - 1)], far_send).wait()
    pltpu.make_async_copy(rest, rest, all_send).wait()


def per_device(
    latents,
    stale_latents,
    edge_latents,
    senders,
    receivers,
    edge_count,
    send_list,
    node_cotangent,
    edge_cotangent,
    edge_first,
    edge_bias,
    edge_second,
    edge_gain,
    node_first,
    node_bias,
    node_second,
    node_gain,
):
    vmem = pl.BlockSpec(memory_space=pltpu.VMEM)
    smem = pl.BlockSpec(memory_space=pltpu.SMEM)
    listed = send_list[0]
    halo = pl.pallas_call(
        halo_kernel,
        out_shape=jax.ShapeDtypeStruct((4 * HALO, W), BF16),
        in_specs=[vmem, vmem],
        out_specs=vmem,
        scratch_shapes=[
            pltpu.VMEM((4, HALO, W), BF16),
            pltpu.VMEM((4, HALO, W), BF16),
            pltpu.SemaphoreType.DMA((4,)),
            pltpu.SemaphoreType.DMA((4,)),
        ],
        compiler_params=pltpu.CompilerParams(
            collective_id=0, has_side_effects=True, vmem_limit_bytes=16 * 2**20
        ),
    )(stale_latents, listed)

    def row(v):
        return v.reshape(1, W)

    def shape(rows, dtype):
        return jax.ShapeDtypeStruct((rows, W), dtype)

    outs = pl.pallas_call(
        layer_kernel,
        out_shape=(
            shape(NODES, BF16),
            shape(NODES, BF16),
            shape(NODES, BF16),
            shape(EDGES, BF16),
            shape(384, F32),
            shape(1, F32),
            shape(128, F32),
            shape(1, F32),
            shape(256, F32),
            shape(1, F32),
            shape(128, F32),
            shape(1, F32),
        ),
        in_specs=[vmem] * 5 + [smem] + [vmem] * 11,
        out_specs=(vmem,) * 12,
        scratch_shapes=[
            pltpu.VMEM((EDGES, 256), BF16),
            pltpu.VMEM((EDGES, 384), BF16),
            pltpu.VMEM((EDGES, W), BF16),
            pltpu.VMEM((EDGES, W), F32),
            pltpu.VMEM((EDGES, W), F32),
            pltpu.VMEM((EDGES, W), F32),
            pltpu.VMEM((EDGES, 256), BF16),
            pltpu.VMEM((EDGES, W), BF16),
            pltpu.VMEM((PACK, W), BF16),
            pltpu.VMEM((NEAR - 1, TILE, W), BF16),
            pltpu.VMEM((TILE, W), BF16),
            pltpu.VMEM((FAR, TILE, W), BF16),
            pltpu.VMEM((TILE, W), BF16),
            pltpu.VMEM((PACK, W), BF16),
            pltpu.VMEM((4, HALO, W), BF16),
            pltpu.VMEM((4, HALO, W), BF16),
        ]
        + [pltpu.SemaphoreType.DMA] * 6
        + [pltpu.SemaphoreType.DMA((4,))] * 2,
        compiler_params=pltpu.CompilerParams(
            collective_id=1, has_side_effects=True, vmem_limit_bytes=48 * 2**20
        ),
    )(
        latents,
        halo,
        edge_latents,
        senders.reshape(EDGES // W, W),
        receivers.reshape(EDGES // W, W),
        edge_count,
        listed,
        node_cotangent,
        edge_cotangent,
        edge_first,
        row(edge_bias),
        edge_second,
        row(edge_gain),
        node_first,
        row(node_bias),
        node_second,
        row(node_gain),
    )
    return tuple(v.reshape(W) if v.shape[0] == 1 else v for v in outs)


def solution(mesh):
    both = ("stream", "cross")
    rows = P(both, None)
    in_specs = (rows, rows, rows, P(both), P(both), P(both), P(both, None, None), rows, rows) + (P(),) * 8
    out_specs = (rows,) * 4 + (P(),) * 8
    return jax.shard_map(
        per_device, mesh=mesh, in_specs=in_specs, out_specs=out_specs, check_vma=False
    )
```

```python
import math

import jax
import jax.numpy as jnp
from jax import lax
from jax.experimental import pallas as pl
from jax.experimental.pallas import tpu as pltpu
from jax.sharding import PartitionSpec as P

EPSILON = 1e-05
MESH = pl.DeviceIdType.MESH
F32 = jnp.float32
BF16 = jnp.bfloat16
W = 128
NODES = 512
EDGES = 1536
HALO = 128
CHUNK = 768
TILE = 32
NEAR = 32
FAR = 16
PACK = TILE * NEAR
ROW_NODE_FIRST = 0
ROW_NODE_SECOND = 256
ROW_EDGE_SECOND = 384
ROW_EDGE_FIRST = 512
ROW_SMALL = 896

CORE = ("s", 1, 2, 0)
Y_HI = ("s", 2, 4, 2)
X = ("s", 8, 4, 1)
Y_LO = ("c", 1, 2, 1)
Z_0 = ("c", 2, 2, 1)
Z_HI = ("c", 4, 4, 2)


class Group:
    def __init__(self, digits, s, c):
        self.s, self.c = s, c
        self.pos = 0
        peers = [(0, 0, 0, 0, 0)]
        size = 1
        for axis, stride, n, apart in digits:
            d = ((s if axis == "s" else c) // stride) % n
            self.pos = self.pos + d * size
            grown = []
            for k in range(n):
                q = (d + k) % n if k else d
                step = (q - d) * stride if k else 0
                for hops, key, ds, dc, at in peers:
                    grown.append(
                        (
                            hops + min(k, n - k) * apart,
                            key + k * size,
                            ds + step if axis == "s" else ds,
                            dc + step if axis == "c" else dc,
                            at + q * size,
                        )
                    )
            peers = grown
            size *= n
        self.size = size
        self.peers = sorted((p for p in peers if p[1]), key=lambda p: (-p[0], p[1]))

    def others(self):
        for _, key, ds, dc, at in self.peers:
            yield key, (self.s + ds, self.c + dc), at


def dot(a, b):
    return jnp.dot(a, b, preferred_element_type=F32)


def dot_nt(a, b):
    return lax.dot_general(a, b, (((1,), (1,)), ((), ())), preferred_element_type=F32)


def dot_tn(a, b):
    return lax.dot_general(a, b, (((0,), (0,)), ((), ())), preferred_element_type=F32)


def columns_of(ref, first, count):
    parts = []
    for k in range(count):
        row = ref[pl.ds(first + k, 1), :]
        parts.append(jnp.broadcast_to(row, (W, W)).T)
    return parts[0] if count == 1 else jnp.concatenate(parts, axis=0)


def hot_rows(col, blocks):
    lane = lax.broadcasted_iota(jnp.int32, col.shape, 1)
    return jnp.concatenate(
        [jnp.where(col == lane + W * j, 1.0, 0.0).astype(BF16) for j in range(blocks)], axis=1
    )


def hot_cols(row, height):
    at = lax.broadcasted_iota(jnp.int32, (height, row.shape[1]), 0)
    return jnp.where(at == row, 1.0, 0.0).astype(BF16)


def sigmoid(v):
    return 0.5 * jnp.tanh(0.5 * v) + 0.5


def normed(z):
    centered = z - jnp.mean(z, axis=-1, keepdims=True)
    rstd = lax.rsqrt(jnp.mean(centered * centered, axis=-1, keepdims=True) + EPSILON)
    return centered * rstd, rstd


def normed_back(dx, xhat, rstd):
    m1 = jnp.mean(dx, axis=-1, keepdims=True)
    m2 = jnp.mean(dx * xhat, axis=-1, keepdims=True)
    return rstd * (dx - m1 - xhat * m2)


def place():
    s = lax.axis_index("stream")
    c = lax.axis_index("cross")
    ns = lax.axis_size("stream")
    nc = lax.axis_size("cross")
    to = [((s + 1, c), s < ns - 1), ((s - 1, c), s > 0), ((s, c + 1), c < nc - 1), ((s, c - 1), c > 0)]
    count = sum(ok.astype(jnp.int32) for _, ok in to)
    return s, c, to, count


BACK = (1, 0, 3, 2)


def first_kernel(
    stale_hbm,
    list_hbm,
    snd_hbm,
    rcv_hbm,
    lat_hbm,
    edge_hbm,
    w1_hbm,
    b1_hbm,
    w2_hbm,
    g_hbm,
    nw1_hbm,
    nb1_hbm,
    nw2_hbm,
    ng_hbm,
    ncot_hbm,
    ecot_hbm,
    count_smem,
    list_ref,
    snd_ref,
    rcv_ref,
    lat_ref,
    edge_ref,
    w1_ref,
    b1_ref,
    w2_ref,
    g_ref,
    nw1_ref,
    nb1_ref,
    nw2_ref,
    ng_ref,
    ncot_ref,
    ecot_ref,
    halo_ref,
    count_ref,
    hot_h_ref,
    hot_r_ref,
    hot_rt_ref,
    rows_s_ref,
    rows_r_ref,
    part_ref,
    stale_ref,
    picked,
    landed,
    load_sem,
    send_sem,
    recv_sem,
):
    s, c, to, count = place()
    barrier = pltpu.get_barrier_semaphore()
    for where, ok in to:

        @pl.when(ok)
        def _(where=where):
            pl.semaphore_signal(barrier, inc=1, device_id=where, device_id_type=MESH)

    pairs = [
        (list_hbm, list_ref),
        (stale_hbm, stale_ref),
        (snd_hbm, snd_ref),
        (rcv_hbm, rcv_ref),
        (lat_hbm, lat_ref),
        (edge_hbm, edge_ref),
        (w1_hbm, w1_ref),
        (b1_hbm, b1_ref),
        (w2_hbm, w2_ref),
        (g_hbm, g_ref),
        (nw1_hbm, nw1_ref),
        (nb1_hbm, nb1_ref),
        (nw2_hbm, nw2_ref),
        (ng_hbm, ng_ref),
        (ncot_hbm, ncot_ref),
        (ecot_hbm, ecot_ref),
    ]
    loads = [pltpu.make_async_copy(a, b, load_sem.at[k]) for k, (a, b) in enumerate(pairs)]
    for load in loads:
        load.start()
    loads[0].wait()
    loads[1].wait()
    table = jnp.concatenate([stale_ref[:256, :], stale_ref[256:, :]], axis=1)
    for k in range(4):
        col = columns_of(list_ref, k, 1)
        both = dot(hot_rows(col & 255, 2), table)
        picked[k] = jnp.where(col < 256, both[:, :W], both[:, W:]).astype(BF16)

    pl.semaphore_wait(barrier, count)

    def copy(k):
        return pltpu.make_async_remote_copy(
            src_ref=picked.at[k],
            dst_ref=landed.at[k],
            send_sem=send_sem.at[k],
            recv_sem=recv_sem.at[k],
            device_id=to[k][0],
            device_id_type=MESH,
        )

    for k in range(4):

        @pl.when(to[k][1])
        def _(k=k):
            copy(k).start()

    for load in loads[2:]:
        load.wait()
    alive_count = count_smem[0]
    count_ref[...] = jnp.full((8, W), alive_count, jnp.int32)
    lat = lat_ref[...]
    per = CHUNK // W
    lane = lax.broadcasted_iota(jnp.int32, (1, W), 1)

    def own_part(i, carry):
        at = pl.ds(pl.multiple_of(i * CHUNK, CHUNK), CHUNK)
        col_s = columns_of(snd_ref, i * per, per)
        col_r = columns_of(rcv_ref, i * per, per)
        row_at = lax.broadcasted_iota(jnp.int32, (CHUNK, W), 0) + i * CHUNK
        hot = hot_rows(jnp.where(row_at < alive_count, col_r, -1), 4)
        hot_r_ref[at, :] = hot
        rows_r = dot(hot, lat).astype(BF16)
        rows_r_ref[at, :] = rows_r
        rows_s = dot(hot_rows(col_s, 4), lat).astype(BF16)
        rows_s_ref[at, :] = rows_s
        hot_h_ref[at, :] = hot_rows(col_s - NODES, 4)
        joined = jnp.concatenate([edge_ref[at, :], rows_s, rows_r], axis=1)
        part_ref[at, :] = dot(joined, w1_ref[...]) + b1_ref[...]
        return carry

    lax.fori_loop(0, EDGES // CHUNK, own_part, 0)
    for k in range(EDGES // W):
        row = jnp.where(lane + k * W < alive_count, rcv_ref[k : k + 1, :], -1)
        hot_rt_ref[:, k * W : (k + 1) * W] = hot_cols(row, NODES)

    for k in range(4):
        has = to[BACK[k]][1]

        @pl.when(has)
        def _(k=k):
            copy(k).wait_recv()
            halo_ref[HALO * k : HALO * (k + 1), :] = landed[k]

        @pl.when(jnp.logical_not(has))
        def _(k=k):
            halo_ref[HALO * k : HALO * (k + 1), :] = jnp.zeros((HALO, W), BF16)

    for k in range(4):

        @pl.when(to[k][1])
        def _(k=k):
            copy(k).wait_send()


def layer_kernel(
    list_ref,
    snd_ref,
    rcv_ref,
    lat_ref,
    edge_ref,
    w1_ref,
    b1_ref,
    w2_ref,
    g_ref,
    nw1_ref,
    nb1_ref,
    nw2_ref,
    ng_ref,
    ncot_ref,
    ecot_ref,
    halo_ref,
    count_ref,
    hot_h_ref,
    hot_r_ref,
    hot_rt_ref,
    rows_s_ref,
    rows_r_ref,
    part_ref,
    new_ref,
    latg_ref,
    staleg_ref,
    edgeg_ref,
    total,
    rows_s,
    hidden,
    slope,
    xhat_s,
    rstd_s,
    values,
    d_recv,
    d_pre,
    pack,
    near_in,
    near_sum,
    far_in,
    far_sum,
    halo_out,
    halo_in,
    near_send,
    near_recv,
    far_send,
    far_recv,
    all_send,
    all_recv,
    halo_send,
    halo_recv,
):
    s, c, to, count = place()
    near = Group((CORE, X, Y_LO, Z_0), s, c)
    far = Group((Y_HI, Z_HI), s, c)
    barrier = pltpu.get_barrier_semaphore()
    for group in (far, near):
        for _, where, _ in group.others():
            pl.semaphore_signal(barrier, inc=1, device_id=where, device_id_type=MESH)
    for where, ok in to:

        @pl.when(ok)
        def _(where=where):
            pl.semaphore_signal(barrier, inc=1, device_id=where, device_id_type=MESH)

    lat = lat_ref[...]
    gain = g_ref[...]
    per = CHUNK // W

    def forward(i, carry):
        at = pl.ds(pl.multiple_of(i * CHUNK, CHUNK), CHUNK)
        rows_h = dot(hot_h_ref[at, :], halo_ref[...]).astype(BF16)
        rows_s[at, :] = rows_s_ref[at, :] + rows_h
        pre = part_ref[at, :] + dot(rows_h, w1_ref[W : 2 * W, :])
        gate = sigmoid(pre)
        act = pre * gate
        slope[at, :] = gate + act * (1.0 - gate)
        act = act.astype(BF16)
        hidden[at, :] = act
        xhat, rstd = normed(dot(act, w2_ref[...]))
        xhat_s[at, :] = xhat
        rstd_s[at, :] = jnp.broadcast_to(rstd, xhat.shape)
        values[at, :W] = (edge_ref[at, :].astype(F32) + xhat * gain).astype(BF16)
        return carry

    lax.fori_loop(0, EDGES // CHUNK, forward, 0)
    agg = dot(hot_rt_ref[...], values[:, :W]).astype(BF16)

    node_in = jnp.concatenate([lat, agg], axis=1)
    pre = dot(node_in, nw1_ref[...]) + nb1_ref[...]
    gate = sigmoid(pre)
    act = pre * gate
    node_slope = gate + act * (1.0 - gate)
    act = act.astype(BF16)
    xhat, rstd = normed(dot(act, nw2_ref[...]))
    ngain = ng_ref[...]
    new_ref[...] = (lat.astype(F32) + xhat * ngain).astype(BF16)
    dy = ncot_ref[...].astype(F32)
    d_ngain = jnp.sum(dy * xhat, axis=0, keepdims=True)
    dz = normed_back(dy * ngain, xhat, rstd).astype(BF16)
    pack[ROW_NODE_SECOND : ROW_NODE_SECOND + 128, :] = dot_tn(act, dz).astype(BF16)
    dp = dot_nt(dz, nw2_ref[...]) * node_slope
    d_nbias = jnp.sum(dp, axis=0, keepdims=True)
    dp = dp.astype(BF16)
    pack[ROW_NODE_FIRST : ROW_NODE_FIRST + 256, :] = dot_tn(node_in, dp).astype(BF16)
    d_in = dot_nt(dp, nw1_ref[...])
    own = dy + d_in[:, :W]
    d_agg = d_in[:, W:].astype(BF16)

    def backward(i, carry):
        d_gain, d_bias = carry
        at = pl.ds(pl.multiple_of(i * CHUNK, CHUNK), CHUNK)
        ct = ecot_ref[at, :].astype(F32) + dot(hot_r_ref[at, :], d_agg)
        row_at = lax.broadcasted_iota(jnp.int32, (CHUNK, W), 0) + i * CHUNK
        dy = jnp.where(row_at < count_ref[0:1, :], ct, 0.0)
        xhat = xhat_s[at, :]
        d_gain = d_gain + jnp.sum(dy * xhat, axis=0, keepdims=True)
        dz = normed_back(dy * gain, xhat, rstd_s[at, :]).astype(BF16)
        dp = dot_nt(dz, w2_ref[...]) * slope[at, :]
        d_bias = d_bias + jnp.sum(dp, axis=0, keepdims=True)
        d_pre[at, :] = dp.astype(BF16)
        xhat_s[at, :] = ct
        values[at, :W] = dz
        return d_gain, d_bias

    zero = jnp.zeros((1, W), F32)
    d_gain, d_bias = lax.fori_loop(0, EDGES // CHUNK, backward, (zero, zero))
    pack[ROW_EDGE_SECOND : ROW_EDGE_SECOND + 128, :] = dot_tn(hidden[...], values[:, :W]).astype(BF16)
    for k, rows in enumerate((edge_ref, rows_s, rows_r_ref)):
        first = ROW_EDGE_FIRST + W * k
        pack[first : first + W, :] = dot_tn(rows[...], d_pre[...]).astype(BF16)
    pack[ROW_SMALL:, :] = jnp.concatenate(
        [d_bias, d_gain, d_nbias, d_ngain, jnp.zeros((PACK - ROW_SMALL - 4, W), F32)], axis=0
    ).astype(BF16)

    pl.semaphore_wait(barrier, count + (NEAR - 1) + (FAR - 1))
    for key, where, at in near.others():
        pltpu.make_async_remote_copy(
            src_ref=pack.at[pl.ds(pl.multiple_of(at * TILE, TILE), TILE)],
            dst_ref=near_in.at[key - 1],
            send_sem=near_send,
            recv_sem=near_recv,
            device_id=where,
            device_id_type=MESH,
        ).start()

    def spread(i, carry):
        at = pl.ds(pl.multiple_of(i * CHUNK, CHUNK), CHUNK)
        d_joined = dot_nt(d_pre[at, :], w1_ref[...])
        edgeg_ref[at, :] = (xhat_s[at, :] + d_joined[:, :W]).astype(BF16)
        mine = columns_of(snd_ref, i * per, per) < 512
        d_s = d_joined[:, W : 2 * W]
        values[at, :] = jnp.concatenate(
            [jnp.where(mine, d_s, 0.0).astype(BF16), jnp.where(mine, 0.0, d_s).astype(BF16)], axis=1
        )
        d_recv[at, :] = d_joined[:, 2 * W :].astype(BF16)
        return carry

    lax.fori_loop(0, EDGES // CHUNK, spread, 0)
    senders = jnp.concatenate([snd_ref[k : k + 1, :] & 511 for k in range(EDGES // W)], axis=1)
    spread_s = dot(hot_cols(senders, 512), values[...])
    for k in range(4):
        halo_out[k] = spread_s[HALO * k : HALO * (k + 1), W:].astype(BF16)

    def back(k):
        return pltpu.make_async_remote_copy(
            src_ref=halo_out.at[k],
            dst_ref=halo_in.at[k],
            send_sem=halo_send.at[k],
            recv_sem=halo_recv.at[k],
            device_id=to[BACK[k]][0],
            device_id_type=MESH,
        )

    for k in range(4):

        @pl.when(to[BACK[k]][1])
        def _(k=k):
            back(k).start()

    spread_r = dot(hot_rt_ref[...], d_recv[...])
    latg_ref[...] = (own + spread_s[:, :W] + spread_r).astype(BF16)

    mine = pl.ds(pl.multiple_of(near.pos * TILE, TILE), TILE)
    pltpu.make_async_copy(near_in, near_in, near_recv).wait()
    acc = pack[mine, :].astype(F32)
    for k in range(NEAR - 1):
        acc = acc + near_in[k].astype(F32)
    near_sum[...] = acc.astype(BF16)
    for key, where, at in far.others():
        pltpu.make_async_remote_copy(
            src_ref=near_sum,
            dst_ref=far_in.at[far.pos],
            send_sem=far_send,
            recv_sem=far_recv,
            device_id=where,
            device_id_type=MESH,
        ).start()

    for k in range(4):
        has = to[k][1]

        @pl.when(has)
        def _(k=k):
            back(k).wait_recv()

        @pl.when(jnp.logical_not(has))
        def _(k=k):
            halo_in[k] = jnp.zeros((HALO, W), BF16)

    parts = []
    for k in range(4):
        low = columns_of(list_ref, k, 1) < 256
        came = halo_in[k].astype(F32)
        parts.append(
            jnp.concatenate(
                [jnp.where(low, came, 0.0).astype(BF16), jnp.where(low, 0.0, came).astype(BF16)],
                axis=1,
            )
        )
    listed = jnp.concatenate([list_ref[k : k + 1, :] & 255 for k in range(4)], axis=1)
    stale = dot(hot_cols(listed, 256), jnp.concatenate(parts, axis=0))
    staleg_ref[...] = jnp.concatenate([stale[:, :W], stale[:, W:]], axis=0).astype(BF16)

    pltpu.make_async_copy(far_in.at[pl.ds(0, FAR - 1)], far_in.at[pl.ds(0, FAR - 1)], far_recv).wait()
    far_in[far.pos] = near_sum[...]
    acc = far_in[0].astype(F32)
    for k in range(1, FAR):
        acc = acc + far_in[k].astype(F32)
    far_sum[...] = acc.astype(BF16)
    for key, where, at in near.others():
        pltpu.make_async_remote_copy(
            src_ref=far_sum,
            dst_ref=total.at[mine],
            send_sem=all_send,
            recv_sem=all_recv,
            device_id=where,
            device_id_type=MESH,
        ).start()
    rest = total.at[pl.ds(0, PACK - TILE)]
    pltpu.make_async_copy(rest, rest, all_recv).wait()
    total[mine, :] = far_sum[...]

    for k in range(4):

        @pl.when(to[BACK[k]][1])
        def _(k=k):
            back(k).wait_send()

    pltpu.make_async_copy(near_in, near_in, near_send).wait()
    pltpu.make_async_copy(far_in.at[pl.ds(0, FAR - 1)], far_in.at[pl.ds(0, FAR - 1)], far_send).wait()
    pltpu.make_async_copy(rest, rest, all_send).wait()


def last_kernel(*refs):
    bulk, total = refs[:4], refs[4]
    outs = refs[5:17]
    scaled, sem = refs[17:25], refs[25]
    copies = [pltpu.make_async_copy(bulk[k], outs[k], sem.at[k]) for k in range(4)]
    for copy in copies:
        copy.start()
    sums = total[...].astype(F32)
    entries = ROW_SMALL * W + 4 * W
    squares = jnp.sum(sums * sums)
    factor = jnp.minimum(1.0, math.sqrt(entries) * lax.rsqrt(jnp.full((1, W), squares, F32)))
    rows = (
        (ROW_EDGE_FIRST, 384),
        (ROW_SMALL, 1),
        (ROW_EDGE_SECOND, 128),
        (ROW_SMALL + 1, 1),
        (ROW_NODE_FIRST, 256),
        (ROW_SMALL + 2, 1),
        (ROW_NODE_SECOND, 128),
        (ROW_SMALL + 3, 1),
    )
    for k, (first, height) in enumerate(rows):
        scaled[k][...] = sums[first : first + height, :] * factor
        copy = pltpu.make_async_copy(scaled[k], outs[4 + k], sem.at[4 + k])
        copy.start()
        copies.append(copy)
    for copy in copies:
        copy.wait()


def per_device(
    latents,
    stale_latents,
    edge_latents,
    senders,
    receivers,
    edge_count,
    send_list,
    node_cotangent,
    edge_cotangent,
    edge_first,
    edge_bias,
    edge_second,
    edge_gain,
    node_first,
    node_bias,
    node_second,
    node_gain,
):
    vmem = pl.BlockSpec(memory_space=pltpu.VMEM)
    hbm = pl.BlockSpec(memory_space=pltpu.HBM)

    def row(v):
        return v.reshape(1, W)

    def far_away(v):
        return pltpu.with_memory_space_constraint(v, pltpu.HBM)

    def shape(rows, dtype, width=W):
        return jax.ShapeDtypeStruct((rows, width), dtype)

    fetched = (
        send_list[0],
        senders.reshape(EDGES // W, W),
        receivers.reshape(EDGES // W, W),
        latents,
        edge_latents,
        edge_first,
        row(edge_bias),
        edge_second,
        row(edge_gain),
        node_first,
        row(node_bias),
        node_second,
        row(node_gain),
        node_cotangent,
        edge_cotangent,
    )
    made = (
        shape(4 * HALO, BF16),
        shape(8, jnp.int32),
        shape(EDGES, BF16, 4 * HALO),
        shape(EDGES, BF16, NODES),
        shape(NODES, BF16, EDGES),
        shape(EDGES, BF16),
        shape(EDGES, BF16),
        shape(EDGES, F32),
    )
    first = pl.pallas_call(
        first_kernel,
        out_shape=tuple(jax.ShapeDtypeStruct(v.shape, v.dtype) for v in fetched) + made,
        in_specs=[hbm] * 16 + [pl.BlockSpec(memory_space=pltpu.SMEM)],
        out_specs=(vmem,) * (len(fetched) + len(made)),
        scratch_shapes=[
            pltpu.VMEM((NODES, W), BF16),
            pltpu.VMEM((4, HALO, W), BF16),
            pltpu.VMEM((4, HALO, W), BF16),
            pltpu.SemaphoreType.DMA((16,)),
            pltpu.SemaphoreType.DMA((4,)),
            pltpu.SemaphoreType.DMA((4,)),
        ],
        compiler_params=pltpu.CompilerParams(
            collective_id=0, has_side_effects=True, vmem_limit_bytes=24 * 2**20
        ),
    )(*(far_away(v) for v in (stale_latents, *fetched)), edge_count)

    second = pl.pallas_call(
        layer_kernel,
        out_shape=(
            shape(NODES, BF16),
            shape(NODES, BF16),
            shape(NODES, BF16),
            shape(EDGES, BF16),
            shape(PACK, BF16),
        ),
        in_specs=[vmem] * len(first),
        out_specs=(vmem,) * 5,
        scratch_shapes=[
            pltpu.VMEM((EDGES, W), BF16),
            pltpu.VMEM((EDGES, W), BF16),
            pltpu.VMEM((EDGES, W), F32),
            pltpu.VMEM((EDGES, W), F32),
            pltpu.VMEM((EDGES, W), F32),
            pltpu.VMEM((EDGES, 256), BF16),
            pltpu.VMEM((EDGES, W), BF16),
            pltpu.VMEM((EDGES, W), BF16),
            pltpu.VMEM((PACK, W), BF16),
            pltpu.VMEM((NEAR - 1, TILE, W), BF16),
            pltpu.VMEM((TILE, W), BF16),
            pltpu.VMEM((FAR, TILE, W), BF16),
            pltpu.VMEM((TILE, W), BF16),
            pltpu.VMEM((4, HALO, W), BF16),
            pltpu.VMEM((4, HALO, W), BF16),
        ]
        + [pltpu.SemaphoreType.DMA] * 6
        + [pltpu.SemaphoreType.DMA((4,))] * 2,
        compiler_params=pltpu.CompilerParams(
            collective_id=1, has_side_effects=True, vmem_limit_bytes=32 * 2**20
        ),
    )(*first)

    weights = (
        shape(384, F32),
        shape(1, F32),
        shape(128, F32),
        shape(1, F32),
        shape(256, F32),
        shape(1, F32),
        shape(128, F32),
        shape(1, F32),
    )
    outs = pl.pallas_call(
        last_kernel,
        out_shape=tuple(jax.ShapeDtypeStruct(v.shape, v.dtype) for v in second[:4]) + weights,
        in_specs=[vmem] * 5,
        out_specs=(hbm,) * 12,
        scratch_shapes=[pltpu.VMEM(v.shape, F32) for v in weights] + [pltpu.SemaphoreType.DMA((12,))],
        compiler_params=pltpu.CompilerParams(vmem_limit_bytes=16 * 2**20),
    )(*second)
    return tuple(v.reshape(W) if v.shape[0] == 1 else v for v in outs)


def solution(mesh):
    both = ("stream", "cross")
    rows = P(both, None)
    in_specs = (rows, rows, rows, P(both), P(both), P(both), P(both, None, None), rows, rows) + (P(),) * 8
    out_specs = (rows,) * 4 + (P(),) * 8
    return jax.shard_map(
        per_device, mesh=mesh, in_specs=in_specs, out_specs=out_specs, check_vma=False
    )
```

```python
import math

import jax
import jax.numpy as jnp
from jax import lax
from jax.experimental import pallas as pl
from jax.experimental.pallas import tpu as pltpu
from jax.sharding import PartitionSpec as P

EPSILON = 1e-05
MESH = pl.DeviceIdType.MESH
F32 = jnp.float32
BF16 = jnp.bfloat16
W = 128
NODES = 512
EDGES = 1536
HALO = 128
CHUNK = 768
TILE = 16
NEAR = 32
FAR = 16
HALF = TILE * NEAR
OWNERS = (32, 25)
PACK = TILE * sum(OWNERS)
ROW_NODE_FIRST = 0
ROW_NODE_SECOND = 256
ROW_EDGE_SECOND = 384
ROW_EDGE_FIRST = 512
ROW_SMALL = 896

CORE = ("s", 1, 2, 0)
Y_HI = ("s", 2, 4, 2)
X = ("s", 8, 4, 1)
Y_LO = ("c", 1, 2, 1)
Z_0 = ("c", 2, 2, 1)
Z_HI = ("c", 4, 4, 2)


class Group:
    def __init__(self, digits, s, c):
        self.s, self.c = s, c
        self.pos = 0
        peers = [(0, 0, 0, 0, 0)]
        size = 1
        for axis, stride, n, apart in digits:
            d = ((s if axis == "s" else c) // stride) % n
            self.pos = self.pos + d * size
            grown = []
            for k in range(n):
                q = (d + k) % n if k else d
                step = (q - d) * stride if k else 0
                for hops, key, ds, dc, at in peers:
                    grown.append(
                        (
                            hops + min(k, n - k) * apart,
                            key + k * size,
                            ds + step if axis == "s" else ds,
                            dc + step if axis == "c" else dc,
                            at + q * size,
                        )
                    )
            peers = grown
            size *= n
        self.size = size
        self.peers = sorted((p for p in peers if p[1]), key=lambda p: (-p[0], p[1]))

    def others(self):
        for _, key, ds, dc, at in self.peers:
            yield key, (self.s + ds, self.c + dc), at


def dot(a, b):
    return jnp.dot(a, b, preferred_element_type=F32)


def dot_nt(a, b):
    return lax.dot_general(a, b, (((1,), (1,)), ((), ())), preferred_element_type=F32)


def dot_tn(a, b):
    return lax.dot_general(a, b, (((0,), (0,)), ((), ())), preferred_element_type=F32)


def columns_of(ref, first, count):
    parts = []
    for k in range(count):
        row = ref[pl.ds(first + k, 1), :]
        parts.append(jnp.broadcast_to(row, (W, W)).T)
    return parts[0] if count == 1 else jnp.concatenate(parts, axis=0)


def hot_rows(col, blocks):
    lane = lax.broadcasted_iota(jnp.int32, col.shape, 1)
    return jnp.concatenate(
        [jnp.where(col == lane + W * j, 1.0, 0.0).astype(BF16) for j in range(blocks)], axis=1
    )


def hot_cols(row, height):
    at = lax.broadcasted_iota(jnp.int32, (height, row.shape[1]), 0)
    return jnp.where(at == row, 1.0, 0.0).astype(BF16)


def sigmoid(v):
    return 0.5 * jnp.tanh(0.5 * v) + 0.5


def normed(z):
    centered = z - jnp.mean(z, axis=-1, keepdims=True)
    rstd = lax.rsqrt(jnp.mean(centered * centered, axis=-1, keepdims=True) + EPSILON)
    return centered * rstd, rstd


def normed_back(dx, xhat, rstd):
    m1 = jnp.mean(dx, axis=-1, keepdims=True)
    m2 = jnp.mean(dx * xhat, axis=-1, keepdims=True)
    return rstd * (dx - m1 - xhat * m2)


def place():
    s = lax.axis_index("stream")
    c = lax.axis_index("cross")
    ns = lax.axis_size("stream")
    nc = lax.axis_size("cross")
    to = [((s + 1, c), s < ns - 1), ((s - 1, c), s > 0), ((s, c + 1), c < nc - 1), ((s, c - 1), c > 0)]
    count = sum(ok.astype(jnp.int32) for _, ok in to)
    return s, c, to, count


BACK = (1, 0, 3, 2)


def first_kernel(
    stale_hbm,
    list_hbm,
    snd_hbm,
    rcv_hbm,
    lat_hbm,
    edge_hbm,
    w1_hbm,
    b1_hbm,
    w2_hbm,
    g_hbm,
    nw1_hbm,
    nb1_hbm,
    nw2_hbm,
    ng_hbm,
    ncot_hbm,
    ecot_hbm,
    count_smem,
    list_ref,
    snd_ref,
    rcv_ref,
    lat_ref,
    edge_ref,
    w1_ref,
    b1_ref,
    w2_ref,
    g_ref,
    nw1_ref,
    nb1_ref,
    nw2_ref,
    ng_ref,
    ncot_ref,
    ecot_ref,
    halo_ref,
    count_ref,
    hot_h_ref,
    hot_r_ref,
    hot_rt_ref,
    rows_s_ref,
    rows_r_ref,
    part_ref,
    stale_ref,
    picked,
    landed,
    load_sem,
    send_sem,
    recv_sem,
):
    s, c, to, count = place()
    barrier = pltpu.get_barrier_semaphore()
    for where, ok in to:

        @pl.when(ok)
        def _(where=where):
            pl.semaphore_signal(barrier, inc=1, device_id=where, device_id_type=MESH)

    pairs = [
        (list_hbm, list_ref),
        (stale_hbm, stale_ref),
        (snd_hbm, snd_ref),
        (rcv_hbm, rcv_ref),
        (lat_hbm, lat_ref),
        (edge_hbm, edge_ref),
        (w1_hbm, w1_ref),
        (b1_hbm, b1_ref),
        (w2_hbm, w2_ref),
        (g_hbm, g_ref),
        (nw1_hbm, nw1_ref),
        (nb1_hbm, nb1_ref),
        (nw2_hbm, nw2_ref),
        (ng_hbm, ng_ref),
        (ncot_hbm, ncot_ref),
        (ecot_hbm, ecot_ref),
    ]
    loads = [pltpu.make_async_copy(a, b, load_sem.at[k]) for k, (a, b) in enumerate(pairs)]
    for load in loads:
        load.start()
    loads[0].wait()
    loads[1].wait()
    table = jnp.concatenate([stale_ref[:256, :], stale_ref[256:, :]], axis=1)
    for k in range(4):
        col = columns_of(list_ref, k, 1)
        both = dot(hot_rows(col & 255, 2), table)
        picked[k] = jnp.where(col < 256, both[:, :W], both[:, W:]).astype(BF16)

    pl.semaphore_wait(barrier, count)

    def copy(k):
        return pltpu.make_async_remote_copy(
            src_ref=picked.at[k],
            dst_ref=landed.at[k],
            send_sem=send_sem.at[k],
            recv_sem=recv_sem.at[k],
            device_id=to[k][0],
            device_id_type=MESH,
        )

    for k in range(4):

        @pl.when(to[k][1])
        def _(k=k):
            copy(k).start()

    for load in loads[2:]:
        load.wait()
    alive_count = count_smem[0]
    count_ref[...] = jnp.full((8, W), alive_count, jnp.int32)
    lat = lat_ref[...]
    per = CHUNK // W
    lane = lax.broadcasted_iota(jnp.int32, (1, W), 1)

    def own_part(i, carry):
        at = pl.ds(pl.multiple_of(i * CHUNK, CHUNK), CHUNK)
        col_s = columns_of(snd_ref, i * per, per)
        col_r = columns_of(rcv_ref, i * per, per)
        row_at = lax.broadcasted_iota(jnp.int32, (CHUNK, W), 0) + i * CHUNK
        hot = hot_rows(jnp.where(row_at < alive_count, col_r, -1), 4)
        hot_r_ref[at, :] = hot
        rows_r = dot(hot, lat).astype(BF16)
        rows_r_ref[at, :] = rows_r
        rows_s = dot(hot_rows(col_s, 4), lat).astype(BF16)
        rows_s_ref[at, :] = rows_s
        hot_h_ref[at, :] = hot_rows(col_s - NODES, 4)
        joined = jnp.concatenate([edge_ref[at, :], rows_s, rows_r], axis=1)
        part_ref[at, :] = dot(joined, w1_ref[...]) + b1_ref[...]
        return carry

    lax.fori_loop(0, EDGES // CHUNK, own_part, 0)
    for k in range(EDGES // W):
        row = jnp.where(lane + k * W < alive_count, rcv_ref[k : k + 1, :], -1)
        hot_rt_ref[:, k * W : (k + 1) * W] = hot_cols(row, NODES)

    for k in range(4):
        has = to[BACK[k]][1]

        @pl.when(has)
        def _(k=k):
            copy(k).wait_recv()
            halo_ref[HALO * k : HALO * (k + 1), :] = landed[k]

        @pl.when(jnp.logical_not(has))
        def _(k=k):
            halo_ref[HALO * k : HALO * (k + 1), :] = jnp.zeros((HALO, W), BF16)

    for k in range(4):

        @pl.when(to[k][1])
        def _(k=k):
            copy(k).wait_send()


def layer_kernel(
    list_ref,
    snd_ref,
    rcv_ref,
    lat_ref,
    edge_ref,
    w1_ref,
    b1_ref,
    w2_ref,
    g_ref,
    nw1_ref,
    nb1_ref,
    nw2_ref,
    ng_ref,
    ncot_ref,
    ecot_ref,
    halo_ref,
    count_ref,
    hot_h_ref,
    hot_r_ref,
    hot_rt_ref,
    rows_s_ref,
    rows_r_ref,
    part_ref,
    new_ref,
    latg_ref,
    staleg_ref,
    edgeg_ref,
    total,
    rows_s,
    hidden,
    slope,
    xhat_s,
    rstd_s,
    values,
    d_recv,
    d_pre,
    pack,
    near_in,
    near_sum,
    far_in,
    far_sum,
    halo_out,
    halo_in,
    near_send,
    near_recv,
    far_send,
    far_recv,
    all_send,
    all_recv,
    halo_send,
    halo_recv,
):
    s, c, to, count = place()
    near = Group((CORE, X, Y_LO, Z_0), s, c)
    far = Group((Y_HI, Z_HI), s, c)
    barrier = pltpu.get_barrier_semaphore()
    for group in (far, near):
        for _, where, _ in group.others():
            pl.semaphore_signal(barrier, inc=1, device_id=where, device_id_type=MESH)
    for where, ok in to:

        @pl.when(ok)
        def _(where=where):
            pl.semaphore_signal(barrier, inc=1, device_id=where, device_id_type=MESH)

    lat = lat_ref[...]
    gain = g_ref[...]
    per = CHUNK // W

    def forward(i, carry):
        at = pl.ds(pl.multiple_of(i * CHUNK, CHUNK), CHUNK)
        rows_h = dot(hot_h_ref[at, :], halo_ref[...]).astype(BF16)
        rows_s[at, :] = rows_s_ref[at, :] + rows_h
        pre = part_ref[at, :] + dot(rows_h, w1_ref[W : 2 * W, :])
        gate = sigmoid(pre)
        act = pre * gate
        slope[at, :] = gate + act * (1.0 - gate)
        act = act.astype(BF16)
        hidden[at, :] = act
        xhat, rstd = normed(dot(act, w2_ref[...]))
        xhat_s[at, :] = xhat
        rstd_s[at, :] = jnp.broadcast_to(rstd, xhat.shape)
        values[at, :W] = (edge_ref[at, :].astype(F32) + xhat * gain).astype(BF16)
        return carry

    lax.fori_loop(0, EDGES // CHUNK, forward, 0)
    agg = dot(hot_rt_ref[...], values[:, :W]).astype(BF16)

    node_in = jnp.concatenate([lat, agg], axis=1)
    pre = dot(node_in, nw1_ref[...]) + nb1_ref[...]
    gate = sigmoid(pre)
    act = pre * gate
    node_slope = gate + act * (1.0 - gate)
    act = act.astype(BF16)
    xhat, rstd = normed(dot(act, nw2_ref[...]))
    ngain = ng_ref[...]
    new_ref[...] = (lat.astype(F32) + xhat * ngain).astype(BF16)
    dy = ncot_ref[...].astype(F32)
    d_ngain = jnp.sum(dy * xhat, axis=0, keepdims=True)
    dz = normed_back(dy * ngain, xhat, rstd).astype(BF16)
    pack[ROW_NODE_SECOND : ROW_NODE_SECOND + 128, :] = dot_tn(act, dz).astype(BF16)
    dp = dot_nt(dz, nw2_ref[...]) * node_slope
    d_nbias = jnp.sum(dp, axis=0, keepdims=True)
    dp = dp.astype(BF16)
    pack[ROW_NODE_FIRST : ROW_NODE_FIRST + 256, :] = dot_tn(node_in, dp).astype(BF16)
    d_in = dot_nt(dp, nw1_ref[...])
    own = dy + d_in[:, :W]
    d_agg = d_in[:, W:].astype(BF16)

    def backward(i, carry):
        d_gain, d_bias = carry
        at = pl.ds(pl.multiple_of(i * CHUNK, CHUNK), CHUNK)
        ct = ecot_ref[at, :].astype(F32) + dot(hot_r_ref[at, :], d_agg)
        row_at = lax.broadcasted_iota(jnp.int32, (CHUNK, W), 0) + i * CHUNK
        dy = jnp.where(row_at < count_ref[0:1, :], ct, 0.0)
        xhat = xhat_s[at, :]
        d_gain = d_gain + jnp.sum(dy * xhat, axis=0, keepdims=True)
        dz = normed_back(dy * gain, xhat, rstd_s[at, :]).astype(BF16)
        dp = dot_nt(dz, w2_ref[...]) * slope[at, :]
        d_bias = d_bias + jnp.sum(dp, axis=0, keepdims=True)
        d_pre[at, :] = dp.astype(BF16)
        xhat_s[at, :] = ct
        values[at, :W] = dz
        return d_gain, d_bias

    zero = jnp.zeros((1, W), F32)
    d_gain, d_bias = lax.fori_loop(0, EDGES // CHUNK, backward, (zero, zero))
    pack[ROW_EDGE_SECOND : ROW_EDGE_SECOND + 128, :] = dot_tn(hidden[...], values[:, :W]).astype(BF16)

    def owner(half, at):
        return at < OWNERS[half]

    def tile(half, at):
        return pl.ds(pl.multiple_of(half * HALF + at * TILE, TILE), TILE)

    def await_tiles(sem, count):
        tiles = pack.at[pl.ds(0, count * TILE)]
        pltpu.make_async_copy(tiles, tiles, sem).wait()

    def near_start(half):
        for key, where, at in near.others():

            @pl.when(owner(half, at))
            def _(key=key, where=where, at=at):
                pltpu.make_async_remote_copy(
                    src_ref=pack.at[tile(half, at)],
                    dst_ref=near_in.at[half, key - 1],
                    send_sem=near_send.at[half],
                    recv_sem=near_recv.at[half],
                    device_id=where,
                    device_id_type=MESH,
                ).start()

    def far_start(half):
        @pl.when(owner(half, near.pos))
        def _():
            await_tiles(near_recv.at[half], NEAR - 1)
            acc = pack[tile(half, near.pos), :].astype(F32)
            for k in range(NEAR - 1):
                acc = acc + near_in[half, k].astype(F32)
            near_sum[half] = acc.astype(BF16)
            for key, where, at in far.others():
                pltpu.make_async_remote_copy(
                    src_ref=near_sum.at[half],
                    dst_ref=far_in.at[half, far.pos],
                    send_sem=far_send.at[half],
                    recv_sem=far_recv.at[half],
                    device_id=where,
                    device_id_type=MESH,
                ).start()

    def all_start(half):
        @pl.when(owner(half, near.pos))
        def _():
            await_tiles(far_recv.at[half], FAR - 1)
            far_in[half, far.pos] = near_sum[half]
            acc = far_in[half, 0].astype(F32)
            for k in range(1, FAR):
                acc = acc + far_in[half, k].astype(F32)
            far_sum[half] = acc.astype(BF16)
            for key, where, at in near.others():
                pltpu.make_async_remote_copy(
                    src_ref=far_sum.at[half],
                    dst_ref=total.at[tile(half, near.pos)],
                    send_sem=all_send.at[half],
                    recv_sem=all_recv.at[half],
                    device_id=where,
                    device_id_type=MESH,
                ).start()
            total[tile(half, near.pos), :] = far_sum[half]

    def await_owners(sem, half):
        @pl.when(owner(half, near.pos))
        def _():
            await_tiles(sem, OWNERS[half] - 1)

        if OWNERS[half] < NEAR:

            @pl.when(jnp.logical_not(owner(half, near.pos)))
            def _():
                await_tiles(sem, OWNERS[half])

    def finish(half):
        await_owners(near_send.at[half], half)

        @pl.when(owner(half, near.pos))
        def _():
            await_tiles(far_send.at[half], FAR - 1)
            await_tiles(all_send.at[half], NEAR - 1)

    pl.semaphore_wait(barrier, count + (NEAR - 1) + (FAR - 1))
    near_start(0)
    for k, rows in enumerate((edge_ref, rows_s, rows_r_ref)):
        first = ROW_EDGE_FIRST + W * k
        pack[first : first + W, :] = dot_tn(rows[...], d_pre[...]).astype(BF16)
    pack[ROW_SMALL:, :] = jnp.concatenate(
        [d_bias, d_gain, d_nbias, d_ngain, jnp.zeros((PACK - ROW_SMALL - 4, W), F32)], axis=0
    ).astype(BF16)
    near_start(1)

    def spread(i, carry):
        at = pl.ds(pl.multiple_of(i * CHUNK, CHUNK), CHUNK)
        d_joined = dot_nt(d_pre[at, :], w1_ref[...])
        edgeg_ref[at, :] = (xhat_s[at, :] + d_joined[:, :W]).astype(BF16)
        mine = columns_of(snd_ref, i * per, per) < 512
        d_s = d_joined[:, W : 2 * W]
        values[at, :] = jnp.concatenate(
            [jnp.where(mine, d_s, 0.0).astype(BF16), jnp.where(mine, 0.0, d_s).astype(BF16)], axis=1
        )
        d_recv[at, :] = d_joined[:, 2 * W :].astype(BF16)
        return carry

    lax.fori_loop(0, EDGES // CHUNK, spread, 0)
    senders = jnp.concatenate([snd_ref[k : k + 1, :] & 511 for k in range(EDGES // W)], axis=1)
    spread_s = dot(hot_cols(senders, 512), values[...])
    for k in range(4):
        halo_out[k] = spread_s[HALO * k : HALO * (k + 1), W:].astype(BF16)

    def back(k):
        return pltpu.make_async_remote_copy(
            src_ref=halo_out.at[k],
            dst_ref=halo_in.at[k],
            send_sem=halo_send.at[k],
            recv_sem=halo_recv.at[k],
            device_id=to[BACK[k]][0],
            device_id_type=MESH,
        )

    for k in range(4):

        @pl.when(to[BACK[k]][1])
        def _(k=k):
            back(k).start()

    spread_r = dot(hot_rt_ref[...], d_recv[...])
    latg_ref[...] = (own + spread_s[:, :W] + spread_r).astype(BF16)

    far_start(0)
    far_start(1)

    for k in range(4):
        has = to[k][1]

        @pl.when(has)
        def _(k=k):
            back(k).wait_recv()

        @pl.when(jnp.logical_not(has))
        def _(k=k):
            halo_in[k] = jnp.zeros((HALO, W), BF16)

    parts = []
    for k in range(4):
        low = columns_of(list_ref, k, 1) < 256
        came = halo_in[k].astype(F32)
        parts.append(
            jnp.concatenate(
                [jnp.where(low, came, 0.0).astype(BF16), jnp.where(low, 0.0, came).astype(BF16)],
                axis=1,
            )
        )
    listed = jnp.concatenate([list_ref[k : k + 1, :] & 255 for k in range(4)], axis=1)
    stale = dot(hot_cols(listed, 256), jnp.concatenate(parts, axis=0))
    staleg_ref[...] = jnp.concatenate([stale[:, :W], stale[:, W:]], axis=0).astype(BF16)

    all_start(0)
    all_start(1)
    for k in range(4):

        @pl.when(to[BACK[k]][1])
        def _(k=k):
            back(k).wait_send()

    await_owners(all_recv.at[0], 0)
    await_owners(all_recv.at[1], 1)
    finish(0)
    finish(1)


def last_kernel(*refs):
    bulk, total = refs[:4], refs[4]
    outs = refs[5:17]
    scaled, sem = refs[17:25], refs[25]
    copies = [pltpu.make_async_copy(bulk[k], outs[k], sem.at[k]) for k in range(4)]
    for copy in copies:
        copy.start()
    sums = total[...].astype(F32)
    entries = ROW_SMALL * W + 4 * W
    squares = jnp.sum(sums * sums)
    factor = jnp.minimum(1.0, math.sqrt(entries) * lax.rsqrt(jnp.full((1, W), squares, F32)))
    rows = (
        (ROW_EDGE_FIRST, 384),
        (ROW_SMALL, 1),
        (ROW_EDGE_SECOND, 128),
        (ROW_SMALL + 1, 1),
        (ROW_NODE_FIRST, 256),
        (ROW_SMALL + 2, 1),
        (ROW_NODE_SECOND, 128),
        (ROW_SMALL + 3, 1),
    )
    for k, (first, height) in enumerate(rows):
        scaled[k][...] = sums[first : first + height, :] * factor
        copy = pltpu.make_async_copy(scaled[k], outs[4 + k], sem.at[4 + k])
        copy.start()
        copies.append(copy)
    for copy in copies:
        copy.wait()


def per_device(
    latents,
    stale_latents,
    edge_latents,
    senders,
    receivers,
    edge_count,
    send_list,
    node_cotangent,
    edge_cotangent,
    edge_first,
    edge_bias,
    edge_second,
    edge_gain,
    node_first,
    node_bias,
    node_second,
    node_gain,
):
    vmem = pl.BlockSpec(memory_space=pltpu.VMEM)
    hbm = pl.BlockSpec(memory_space=pltpu.HBM)

    def row(v):
        return v.reshape(1, W)

    def far_away(v):
        return pltpu.with_memory_space_constraint(v, pltpu.HBM)

    def shape(rows, dtype, width=W):
        return jax.ShapeDtypeStruct((rows, width), dtype)

    fetched = (
        send_list[0],
        senders.reshape(EDGES // W, W),
        receivers.reshape(EDGES // W, W),
        latents,
        edge_latents,
        edge_first,
        row(edge_bias),
        edge_second,
        row(edge_gain),
        node_first,
        row(node_bias),
        node_second,
        row(node_gain),
        node_cotangent,
        edge_cotangent,
    )
    made = (
        shape(4 * HALO, BF16),
        shape(8, jnp.int32),
        shape(EDGES, BF16, 4 * HALO),
        shape(EDGES, BF16, NODES),
        shape(NODES, BF16, EDGES),
        shape(EDGES, BF16),
        shape(EDGES, BF16),
        shape(EDGES, F32),
    )
    first = pl.pallas_call(
        first_kernel,
        out_shape=tuple(jax.ShapeDtypeStruct(v.shape, v.dtype) for v in fetched) + made,
        in_specs=[hbm] * 16 + [pl.BlockSpec(memory_space=pltpu.SMEM)],
        out_specs=(vmem,) * (len(fetched) + len(made)),
        scratch_shapes=[
            pltpu.VMEM((NODES, W), BF16),
            pltpu.VMEM((4, HALO, W), BF16),
            pltpu.VMEM((4, HALO, W), BF16),
            pltpu.SemaphoreType.DMA((16,)),
            pltpu.SemaphoreType.DMA((4,)),
            pltpu.SemaphoreType.DMA((4,)),
        ],
        compiler_params=pltpu.CompilerParams(
            collective_id=0, has_side_effects=True, vmem_limit_bytes=24 * 2**20
        ),
    )(*(far_away(v) for v in (stale_latents, *fetched)), edge_count)

    second = pl.pallas_call(
        layer_kernel,
        out_shape=(
            shape(NODES, BF16),
            shape(NODES, BF16),
            shape(NODES, BF16),
            shape(EDGES, BF16),
            shape(PACK, BF16),
        ),
        in_specs=[vmem] * len(first),
        out_specs=(vmem,) * 5,
        scratch_shapes=[
            pltpu.VMEM((EDGES, W), BF16),
            pltpu.VMEM((EDGES, W), BF16),
            pltpu.VMEM((EDGES, W), F32),
            pltpu.VMEM((EDGES, W), F32),
            pltpu.VMEM((EDGES, W), F32),
            pltpu.VMEM((EDGES, 256), BF16),
            pltpu.VMEM((EDGES, W), BF16),
            pltpu.VMEM((EDGES, W), BF16),
            pltpu.VMEM((PACK, W), BF16),
            pltpu.VMEM((2, NEAR - 1, TILE, W), BF16),
            pltpu.VMEM((2, TILE, W), BF16),
            pltpu.VMEM((2, FAR, TILE, W), BF16),
            pltpu.VMEM((2, TILE, W), BF16),
            pltpu.VMEM((4, HALO, W), BF16),
            pltpu.VMEM((4, HALO, W), BF16),
        ]
        + [pltpu.SemaphoreType.DMA((2,))] * 6
        + [pltpu.SemaphoreType.DMA((4,))] * 2,
        compiler_params=pltpu.CompilerParams(
            collective_id=1, has_side_effects=True, vmem_limit_bytes=32 * 2**20
        ),
    )(*first)

    weights = (
        shape(384, F32),
        shape(1, F32),
        shape(128, F32),
        shape(1, F32),
        shape(256, F32),
        shape(1, F32),
        shape(128, F32),
        shape(1, F32),
    )
    outs = pl.pallas_call(
        last_kernel,
        out_shape=tuple(jax.ShapeDtypeStruct(v.shape, v.dtype) for v in second[:4]) + weights,
        in_specs=[vmem] * 5,
        out_specs=(hbm,) * 12,
        scratch_shapes=[pltpu.VMEM(v.shape, F32) for v in weights] + [pltpu.SemaphoreType.DMA((12,))],
        compiler_params=pltpu.CompilerParams(vmem_limit_bytes=16 * 2**20),
    )(*second)
    return tuple(v.reshape(W) if v.shape[0] == 1 else v for v in outs)


def solution(mesh):
    both = ("stream", "cross")
    rows = P(both, None)
    in_specs = (rows, rows, rows, P(both), P(both), P(both), P(both, None, None), rows, rows) + (P(),) * 8
    out_specs = (rows,) * 4 + (P(),) * 8
    return jax.shard_map(
        per_device, mesh=mesh, in_specs=in_specs, out_specs=out_specs, check_vma=False
    )
```

```python
import math

import jax
import jax.numpy as jnp
from jax import lax
from jax.experimental import pallas as pl
from jax.experimental.pallas import tpu as pltpu
from jax.sharding import PartitionSpec as P

EPSILON = 1e-05
MESH = pl.DeviceIdType.MESH
F32 = jnp.float32
BF16 = jnp.bfloat16
W = 128
NODES = 512
EDGES = 1536
HALO = 128
CHUNK = 1536
TILE = 16
NEAR = 32
FAR = 16
HALF = TILE * NEAR
OWNERS = (32, 25)
PACK = TILE * sum(OWNERS)
ROW_NODE_FIRST = 0
ROW_NODE_SECOND = 256
ROW_EDGE_SECOND = 384
ROW_EDGE_FIRST = 512
ROW_SMALL = 896


def ring_pair(p):
    pair = ((p + 1) // 2) % 4
    turned = ((pair + 1) // 2 + 1) % 2
    return pair, ((p + 1) % 2 + turned) % 2


def ring_place(pair, label):
    turned = ((pair + 1) // 2 + 1) % 2
    return (2 * pair + (label + turned) % 2 + 7) % 8


class Peers:
    def __init__(self, s, c):
        core, x = s % 2, s // 8
        y, z = ((s // 2) % 4) * 2 + c % 2, c // 2
        (wy, ly), (wz, lz) = ring_pair(y), ring_pair(z)
        cores = [core, 1 - core]
        xs = [(x + k) % 4 for k in range(4)]
        self.near_pos = core + 2 * x + 8 * ly + 16 * lz
        self.far_pos = wy + 4 * wz
        ys = [(y, ly), (ring_place(wy, 1 - ly), 1 - ly)]
        zs = [(z, lz), (ring_place(wz, 1 - lz), 1 - lz)]
        near = []
        for kc in range(2):
            for kx in range(4):
                for ky in range(2):
                    for kz in range(2):
                        key = kc + 2 * kx + 8 * ky + 16 * kz
                        hops = (0, 1, 2, 1)[kx] + ky + kz
                        (py, qy), (pz, qz) = ys[ky], zs[kz]
                        at = cores[kc] + 2 * xs[kx] + 8 * qy + 16 * qz
                        near.append((-hops, key, self.device(xs[kx], py, pz, cores[kc]), at))
        far = []
        for ky in range(4):
            for kz in range(4):
                key = ky + 4 * kz
                hops = (0, 2, 3, 2)[ky] + (0, 2, 3, 2)[kz]
                py = ring_place((wy + ky) % 4, ly) if ky else y
                pz = ring_place((wz + kz) % 4, lz) if kz else z
                far.append((-hops, key, self.device(x, py, pz, core)))
        self.near = [p[1:] for p in sorted(near, key=lambda p: p[:2]) if p[1]]
        self.far = [p[1:] for p in sorted(far, key=lambda p: p[:2]) if p[1]]

    @staticmethod
    def device(x, y, z, core):
        return 8 * x + 2 * (y // 2) + core, 2 * z + y % 2


def dot(a, b):
    return jnp.dot(a, b, preferred_element_type=F32)


def dot_nt(a, b):
    return lax.dot_general(a, b, (((1,), (1,)), ((), ())), preferred_element_type=F32)


def dot_tn(a, b):
    return lax.dot_general(a, b, (((0,), (0,)), ((), ())), preferred_element_type=F32)


def columns_of(ref, first, count):
    parts = []
    for k in range(count):
        row = ref[pl.ds(first + k, 1), :]
        parts.append(jnp.broadcast_to(row, (W, W)).T)
    return parts[0] if count == 1 else jnp.concatenate(parts, axis=0)


def hot_rows(col, blocks):
    lane = lax.broadcasted_iota(jnp.int32, col.shape, 1)
    return jnp.concatenate(
        [jnp.where(col == lane + W * j, 1.0, 0.0).astype(BF16) for j in range(blocks)], axis=1
    )


def hot_cols(row, height):
    at = lax.broadcasted_iota(jnp.int32, (height, row.shape[1]), 0)
    return jnp.where(at == row, 1.0, 0.0).astype(BF16)


def sigmoid(v):
    return 0.5 * jnp.tanh(0.5 * v) + 0.5


def normed(z):
    centered = z - jnp.mean(z, axis=-1, keepdims=True)
    rstd = lax.rsqrt(jnp.mean(centered * centered, axis=-1, keepdims=True) + EPSILON)
    return centered * rstd, rstd


def normed_back(dx, xhat, rstd):
    m1 = jnp.mean(dx, axis=-1, keepdims=True)
    m2 = jnp.mean(dx * xhat, axis=-1, keepdims=True)
    return rstd * (dx - m1 - xhat * m2)


def place():
    s = lax.axis_index("stream")
    c = lax.axis_index("cross")
    ns = lax.axis_size("stream")
    nc = lax.axis_size("cross")
    to = [((s + 1, c), s < ns - 1), ((s - 1, c), s > 0), ((s, c + 1), c < nc - 1), ((s, c - 1), c > 0)]
    count = sum(ok.astype(jnp.int32) for _, ok in to)
    return s, c, to, count


BACK = (1, 0, 3, 2)


def first_kernel(
    stale_hbm,
    list_hbm,
    snd_hbm,
    rcv_hbm,
    lat_hbm,
    edge_hbm,
    w1_hbm,
    b1_hbm,
    w2_hbm,
    g_hbm,
    nw1_hbm,
    nb1_hbm,
    nw2_hbm,
    ng_hbm,
    ncot_hbm,
    ecot_hbm,
    count_smem,
    list_ref,
    snd_ref,
    rcv_ref,
    lat_ref,
    edge_ref,
    w1_ref,
    b1_ref,
    w2_ref,
    g_ref,
    nw1_ref,
    nb1_ref,
    nw2_ref,
    ng_ref,
    ncot_ref,
    ecot_ref,
    halo_ref,
    count_ref,
    hot_h_ref,
    hot_r_ref,
    hot_rt_ref,
    rows_s_ref,
    rows_r_ref,
    part_ref,
    stale_ref,
    picked,
    landed,
    load_sem,
    send_sem,
    recv_sem,
):
    s, c, to, count = place()
    barrier = pltpu.get_barrier_semaphore()
    for where, ok in to:

        @pl.when(ok)
        def _(where=where):
            pl.semaphore_signal(barrier, inc=1, device_id=where, device_id_type=MESH)

    pairs = [
        (list_hbm, list_ref),
        (stale_hbm, stale_ref),
        (snd_hbm, snd_ref),
        (rcv_hbm, rcv_ref),
        (lat_hbm, lat_ref),
        (edge_hbm, edge_ref),
        (w1_hbm, w1_ref),
        (b1_hbm, b1_ref),
        (w2_hbm, w2_ref),
        (g_hbm, g_ref),
        (nw1_hbm, nw1_ref),
        (nb1_hbm, nb1_ref),
        (nw2_hbm, nw2_ref),
        (ng_hbm, ng_ref),
        (ncot_hbm, ncot_ref),
        (ecot_hbm, ecot_ref),
    ]
    loads = [pltpu.make_async_copy(a, b, load_sem.at[k]) for k, (a, b) in enumerate(pairs)]
    for load in loads:
        load.start()
    loads[0].wait()
    loads[1].wait()
    table = jnp.concatenate([stale_ref[:256, :], stale_ref[256:, :]], axis=1)
    for k in range(4):
        col = columns_of(list_ref, k, 1)
        both = dot(hot_rows(col & 255, 2), table)
        picked[k] = jnp.where(col < 256, both[:, :W], both[:, W:]).astype(BF16)

    pl.semaphore_wait(barrier, count)

    def copy(k):
        return pltpu.make_async_remote_copy(
            src_ref=picked.at[k],
            dst_ref=landed.at[k],
            send_sem=send_sem.at[k],
            recv_sem=recv_sem.at[k],
            device_id=to[k][0],
            device_id_type=MESH,
        )

    for k in range(4):

        @pl.when(to[k][1])
        def _(k=k):
            copy(k).start()

    for load in loads[2:]:
        load.wait()
    alive_count = count_smem[0]
    count_ref[...] = jnp.full((8, W), alive_count, jnp.int32)
    lat = lat_ref[...]
    per = CHUNK // W
    lane = lax.broadcasted_iota(jnp.int32, (1, W), 1)

    def own_part(i, carry):
        at = pl.ds(pl.multiple_of(i * CHUNK, CHUNK), CHUNK)
        col_s = columns_of(snd_ref, i * per, per)
        col_r = columns_of(rcv_ref, i * per, per)
        row_at = lax.broadcasted_iota(jnp.int32, (CHUNK, W), 0) + i * CHUNK
        hot = hot_rows(jnp.where(row_at < alive_count, col_r, -1), 4)
        hot_r_ref[at, :] = hot
        rows_r = dot(hot, lat).astype(BF16)
        rows_r_ref[at, :] = rows_r
        rows_s = dot(hot_rows(col_s, 4), lat).astype(BF16)
        rows_s_ref[at, :] = rows_s
        hot_h_ref[at, :] = hot_rows(col_s - NODES, 4)
        joined = jnp.concatenate([edge_ref[at, :], rows_s, rows_r], axis=1)
        part_ref[at, :] = dot(joined, w1_ref[...]) + b1_ref[...]
        return carry

    lax.fori_loop(0, EDGES // CHUNK, own_part, 0)
    for k in range(EDGES // W):
        row = jnp.where(lane + k * W < alive_count, rcv_ref[k : k + 1, :], -1)
        hot_rt_ref[:, k * W : (k + 1) * W] = hot_cols(row, NODES)

    for k in range(4):
        has = to[BACK[k]][1]

        @pl.when(has)
        def _(k=k):
            copy(k).wait_recv()
            halo_ref[HALO * k : HALO * (k + 1), :] = landed[k]

        @pl.when(jnp.logical_not(has))
        def _(k=k):
            halo_ref[HALO * k : HALO * (k + 1), :] = jnp.zeros((HALO, W), BF16)

    for k in range(4):

        @pl.when(to[k][1])
        def _(k=k):
            copy(k).wait_send()


def layer_kernel(
    list_ref,
    snd_ref,
    rcv_ref,
    lat_ref,
    edge_ref,
    w1_ref,
    b1_ref,
    w2_ref,
    g_ref,
    nw1_ref,
    nb1_ref,
    nw2_ref,
    ng_ref,
    ncot_ref,
    ecot_ref,
    halo_ref,
    count_ref,
    hot_h_ref,
    hot_r_ref,
    hot_rt_ref,
    rows_s_ref,
    rows_r_ref,
    part_ref,
    new_ref,
    latg_ref,
    staleg_ref,
    edgeg_ref,
    total,
    rows_s,
    hidden,
    slope,
    xhat_s,
    rstd_s,
    values,
    d_recv,
    d_pre,
    pack,
    near_in,
    near_sum,
    far_in,
    far_sum,
    halo_out,
    halo_in,
    near_send,
    near_recv,
    far_send,
    far_recv,
    all_send,
    all_recv,
    halo_send,
    halo_recv,
):
    s, c, to, count = place()
    peers = Peers(s, c)
    barrier = pltpu.get_barrier_semaphore()
    for peer in peers.far + peers.near:
        pl.semaphore_signal(barrier, inc=1, device_id=peer[1], device_id_type=MESH)
    for where, ok in to:

        @pl.when(ok)
        def _(where=where):
            pl.semaphore_signal(barrier, inc=1, device_id=where, device_id_type=MESH)

    lat = lat_ref[...]
    gain = g_ref[...]
    per = CHUNK // W

    def forward(i, carry):
        at = pl.ds(pl.multiple_of(i * CHUNK, CHUNK), CHUNK)
        rows_h = dot(hot_h_ref[at, :], halo_ref[...]).astype(BF16)
        rows_s[at, :] = rows_s_ref[at, :] + rows_h
        pre = part_ref[at, :] + dot(rows_h, w1_ref[W : 2 * W, :])
        gate = sigmoid(pre)
        act = pre * gate
        slope[at, :] = gate + act * (1.0 - gate)
        act = act.astype(BF16)
        hidden[at, :] = act
        xhat, rstd = normed(dot(act, w2_ref[...]))
        xhat_s[at, :] = xhat
        rstd_s[at, :] = jnp.broadcast_to(rstd, xhat.shape)
        values[at, :W] = (edge_ref[at, :].astype(F32) + xhat * gain).astype(BF16)
        return carry

    lax.fori_loop(0, EDGES // CHUNK, forward, 0)
    agg = dot(hot_rt_ref[...], values[:, :W]).astype(BF16)

    node_in = jnp.concatenate([lat, agg], axis=1)
    pre = dot(node_in, nw1_ref[...]) + nb1_ref[...]
    gate = sigmoid(pre)
    act = pre * gate
    node_slope = gate + act * (1.0 - gate)
    act = act.astype(BF16)
    xhat, rstd = normed(dot(act, nw2_ref[...]))
    ngain = ng_ref[...]
    new_ref[...] = (lat.astype(F32) + xhat * ngain).astype(BF16)
    dy = ncot_ref[...].astype(F32)
    d_ngain = jnp.sum(dy * xhat, axis=0, keepdims=True)
    dz = normed_back(dy * ngain, xhat, rstd).astype(BF16)
    pack[ROW_NODE_SECOND : ROW_NODE_SECOND + 128, :] = dot_tn(act, dz).astype(BF16)
    dp = dot_nt(dz, nw2_ref[...]) * node_slope
    d_nbias = jnp.sum(dp, axis=0, keepdims=True)
    dp = dp.astype(BF16)
    pack[ROW_NODE_FIRST : ROW_NODE_FIRST + 256, :] = dot_tn(node_in, dp).astype(BF16)
    d_in = dot_nt(dp, nw1_ref[...])
    own = dy + d_in[:, :W]
    d_agg = d_in[:, W:].astype(BF16)

    def backward(i, carry):
        d_gain, d_bias = carry
        at = pl.ds(pl.multiple_of(i * CHUNK, CHUNK), CHUNK)
        ct = ecot_ref[at, :].astype(F32) + dot(hot_r_ref[at, :], d_agg)
        row_at = lax.broadcasted_iota(jnp.int32, (CHUNK, W), 0) + i * CHUNK
        dy = jnp.where(row_at < count_ref[0:1, :], ct, 0.0)
        xhat = xhat_s[at, :]
        d_gain = d_gain + jnp.sum(dy * xhat, axis=0, keepdims=True)
        dz = normed_back(dy * gain, xhat, rstd_s[at, :]).astype(BF16)
        dp = dot_nt(dz, w2_ref[...]) * slope[at, :]
        d_bias = d_bias + jnp.sum(dp, axis=0, keepdims=True)
        d_pre[at, :] = dp.astype(BF16)
        xhat_s[at, :] = ct
        values[at, :W] = dz
        return d_gain, d_bias

    zero = jnp.zeros((1, W), F32)
    d_gain, d_bias = lax.fori_loop(0, EDGES // CHUNK, backward, (zero, zero))
    pack[ROW_EDGE_SECOND : ROW_EDGE_SECOND + 128, :] = dot_tn(hidden[...], values[:, :W]).astype(BF16)

    def owner(half, at):
        return at < OWNERS[half]

    def tile(half, at):
        return pl.ds(pl.multiple_of(half * HALF + at * TILE, TILE), TILE)

    def await_tiles(sem, count):
        tiles = pack.at[pl.ds(0, count * TILE)]
        pltpu.make_async_copy(tiles, tiles, sem).wait()

    def near_start(half):
        for key, where, at in peers.near:

            @pl.when(owner(half, at))
            def _(key=key, where=where, at=at):
                pltpu.make_async_remote_copy(
                    src_ref=pack.at[tile(half, at)],
                    dst_ref=near_in.at[half, key - 1],
                    send_sem=near_send.at[half],
                    recv_sem=near_recv.at[half],
                    device_id=where,
                    device_id_type=MESH,
                ).start()

    def far_start(half):
        @pl.when(owner(half, peers.near_pos))
        def _():
            await_tiles(near_recv.at[half], NEAR - 1)
            acc = pack[tile(half, peers.near_pos), :].astype(F32)
            for k in range(NEAR - 1):
                acc = acc + near_in[half, k].astype(F32)
            near_sum[half] = acc.astype(BF16)
            for key, where in peers.far:
                pltpu.make_async_remote_copy(
                    src_ref=near_sum.at[half],
                    dst_ref=far_in.at[half, peers.far_pos],
                    send_sem=far_send.at[half],
                    recv_sem=far_recv.at[half],
                    device_id=where,
                    device_id_type=MESH,
                ).start()

    def all_start(half):
        @pl.when(owner(half, peers.near_pos))
        def _():
            await_tiles(far_recv.at[half], FAR - 1)
            far_in[half, peers.far_pos] = near_sum[half]
            acc = far_in[half, 0].astype(F32)
            for k in range(1, FAR):
                acc = acc + far_in[half, k].astype(F32)
            far_sum[half] = acc.astype(BF16)
            for key, where, at in peers.near:
                pltpu.make_async_remote_copy(
                    src_ref=far_sum.at[half],
                    dst_ref=total.at[tile(half, peers.near_pos)],
                    send_sem=all_send.at[half],
                    recv_sem=all_recv.at[half],
                    device_id=where,
                    device_id_type=MESH,
                ).start()
            total[tile(half, peers.near_pos), :] = far_sum[half]

    def await_owners(sem, half):
        @pl.when(owner(half, peers.near_pos))
        def _():
            await_tiles(sem, OWNERS[half] - 1)

        if OWNERS[half] < NEAR:

            @pl.when(jnp.logical_not(owner(half, peers.near_pos)))
            def _():
                await_tiles(sem, OWNERS[half])

    def finish(half):
        await_owners(near_send.at[half], half)

        @pl.when(owner(half, peers.near_pos))
        def _():
            await_tiles(far_send.at[half], FAR - 1)
            await_tiles(all_send.at[half], NEAR - 1)

    pl.semaphore_wait(barrier, count + (NEAR - 1) + (FAR - 1))
    near_start(0)
    for k, rows in enumerate((edge_ref, rows_s, rows_r_ref)):
        first = ROW_EDGE_FIRST + W * k
        pack[first : first + W, :] = dot_tn(rows[...], d_pre[...]).astype(BF16)
    pack[ROW_SMALL:, :] = jnp.concatenate(
        [d_bias, d_gain, d_nbias, d_ngain, jnp.zeros((PACK - ROW_SMALL - 4, W), F32)], axis=0
    ).astype(BF16)
    near_start(1)

    def spread(i, carry):
        at = pl.ds(pl.multiple_of(i * CHUNK, CHUNK), CHUNK)
        d_joined = dot_nt(d_pre[at, :], w1_ref[...])
        edgeg_ref[at, :] = (xhat_s[at, :] + d_joined[:, :W]).astype(BF16)
        mine = columns_of(snd_ref, i * per, per) < 512
        d_s = d_joined[:, W : 2 * W]
        values[at, :] = jnp.concatenate(
            [jnp.where(mine, d_s, 0.0).astype(BF16), jnp.where(mine, 0.0, d_s).astype(BF16)], axis=1
        )
        d_recv[at, :] = d_joined[:, 2 * W :].astype(BF16)
        return carry

    lax.fori_loop(0, EDGES // CHUNK, spread, 0)
    senders = jnp.concatenate([snd_ref[k : k + 1, :] & 511 for k in range(EDGES // W)], axis=1)
    spread_s = dot(hot_cols(senders, 512), values[...])
    for k in range(4):
        halo_out[k] = spread_s[HALO * k : HALO * (k + 1), W:].astype(BF16)

    def back(k):
        return pltpu.make_async_remote_copy(
            src_ref=halo_out.at[k],
            dst_ref=halo_in.at[k],
            send_sem=halo_send.at[k],
            recv_sem=halo_recv.at[k],
            device_id=to[BACK[k]][0],
            device_id_type=MESH,
        )

    for k in range(4):

        @pl.when(to[BACK[k]][1])
        def _(k=k):
            back(k).start()

    spread_r = dot(hot_rt_ref[...], d_recv[...])
    latg_ref[...] = (own + spread_s[:, :W] + spread_r).astype(BF16)

    far_start(0)
    far_start(1)

    for k in range(4):
        has = to[k][1]

        @pl.when(has)
        def _(k=k):
            back(k).wait_recv()

        @pl.when(jnp.logical_not(has))
        def _(k=k):
            halo_in[k] = jnp.zeros((HALO, W), BF16)

    parts = []
    for k in range(4):
        low = columns_of(list_ref, k, 1) < 256
        came = halo_in[k].astype(F32)
        parts.append(
            jnp.concatenate(
                [jnp.where(low, came, 0.0).astype(BF16), jnp.where(low, 0.0, came).astype(BF16)],
                axis=1,
            )
        )
    listed = jnp.concatenate([list_ref[k : k + 1, :] & 255 for k in range(4)], axis=1)
    stale = dot(hot_cols(listed, 256), jnp.concatenate(parts, axis=0))
    staleg_ref[...] = jnp.concatenate([stale[:, :W], stale[:, W:]], axis=0).astype(BF16)

    all_start(0)
    all_start(1)
    for k in range(4):

        @pl.when(to[BACK[k]][1])
        def _(k=k):
            back(k).wait_send()

    await_owners(all_recv.at[0], 0)
    await_owners(all_recv.at[1], 1)
    finish(0)
    finish(1)


def last_kernel(*refs):
    bulk, total = refs[:4], refs[4]
    outs = refs[5:17]
    scaled, sem = refs[17:25], refs[25]
    copies = [pltpu.make_async_copy(bulk[k], outs[k], sem.at[k]) for k in range(4)]
    for copy in copies:
        copy.start()
    sums = total[...].astype(F32)
    entries = ROW_SMALL * W + 4 * W
    squares = jnp.sum(sums * sums)
    factor = jnp.minimum(1.0, math.sqrt(entries) * lax.rsqrt(jnp.full((1, W), squares, F32)))
    rows = (
        (ROW_EDGE_FIRST, 384),
        (ROW_SMALL, 1),
        (ROW_EDGE_SECOND, 128),
        (ROW_SMALL + 1, 1),
        (ROW_NODE_FIRST, 256),
        (ROW_SMALL + 2, 1),
        (ROW_NODE_SECOND, 128),
        (ROW_SMALL + 3, 1),
    )
    for k, (first, height) in enumerate(rows):
        scaled[k][...] = sums[first : first + height, :] * factor
        copy = pltpu.make_async_copy(scaled[k], outs[4 + k], sem.at[4 + k])
        copy.start()
        copies.append(copy)
    for copy in copies:
        copy.wait()


def per_device(
    latents,
    stale_latents,
    edge_latents,
    senders,
    receivers,
    edge_count,
    send_list,
    node_cotangent,
    edge_cotangent,
    edge_first,
    edge_bias,
    edge_second,
    edge_gain,
    node_first,
    node_bias,
    node_second,
    node_gain,
):
    vmem = pl.BlockSpec(memory_space=pltpu.VMEM)
    hbm = pl.BlockSpec(memory_space=pltpu.HBM)

    def row(v):
        return v.reshape(1, W)

    def far_away(v):
        return pltpu.with_memory_space_constraint(v, pltpu.HBM)

    def shape(rows, dtype, width=W):
        return jax.ShapeDtypeStruct((rows, width), dtype)

    fetched = (
        send_list[0],
        senders.reshape(EDGES // W, W),
        receivers.reshape(EDGES // W, W),
        latents,
        edge_latents,
        edge_first,
        row(edge_bias),
        edge_second,
        row(edge_gain),
        node_first,
        row(node_bias),
        node_second,
        row(node_gain),
        node_cotangent,
        edge_cotangent,
    )
    made = (
        shape(4 * HALO, BF16),
        shape(8, jnp.int32),
        shape(EDGES, BF16, 4 * HALO),
        shape(EDGES, BF16, NODES),
        shape(NODES, BF16, EDGES),
        shape(EDGES, BF16),
        shape(EDGES, BF16),
        shape(EDGES, F32),
    )
    first = pl.pallas_call(
        first_kernel,
        out_shape=tuple(jax.ShapeDtypeStruct(v.shape, v.dtype) for v in fetched) + made,
        in_specs=[hbm] * 16 + [pl.BlockSpec(memory_space=pltpu.SMEM)],
        out_specs=(vmem,) * (len(fetched) + len(made)),
        scratch_shapes=[
            pltpu.VMEM((NODES, W), BF16),
            pltpu.VMEM((4, HALO, W), BF16),
            pltpu.VMEM((4, HALO, W), BF16),
            pltpu.SemaphoreType.DMA((16,)),
            pltpu.SemaphoreType.DMA((4,)),
            pltpu.SemaphoreType.DMA((4,)),
        ],
        compiler_params=pltpu.CompilerParams(
            collective_id=0, has_side_effects=True, vmem_limit_bytes=24 * 2**20
        ),
    )(*(far_away(v) for v in (stale_latents, *fetched)), edge_count)

    second = pl.pallas_call(
        layer_kernel,
        out_shape=(
            shape(NODES, BF16),
            shape(NODES, BF16),
            shape(NODES, BF16),
            shape(EDGES, BF16),
            shape(PACK, BF16),
        ),
        in_specs=[vmem] * len(first),
        out_specs=(vmem,) * 5,
        scratch_shapes=[
            pltpu.VMEM((EDGES, W), BF16),
            pltpu.VMEM((EDGES, W), BF16),
            pltpu.VMEM((EDGES, W), F32),
            pltpu.VMEM((EDGES, W), F32),
            pltpu.VMEM((EDGES, W), F32),
            pltpu.VMEM((EDGES, 256), BF16),
            pltpu.VMEM((EDGES, W), BF16),
            pltpu.VMEM((EDGES, W), BF16),
            pltpu.VMEM((PACK, W), BF16),
            pltpu.VMEM((2, NEAR - 1, TILE, W), BF16),
            pltpu.VMEM((2, TILE, W), BF16),
            pltpu.VMEM((2, FAR, TILE, W), BF16),
            pltpu.VMEM((2, TILE, W), BF16),
            pltpu.VMEM((4, HALO, W), BF16),
            pltpu.VMEM((4, HALO, W), BF16),
        ]
        + [pltpu.SemaphoreType.DMA((2,))] * 6
        + [pltpu.SemaphoreType.DMA((4,))] * 2,
        compiler_params=pltpu.CompilerParams(
            collective_id=1, has_side_effects=True, vmem_limit_bytes=32 * 2**20
        ),
    )(*first)

    weights = (
        shape(384, F32),
        shape(1, F32),
        shape(128, F32),
        shape(1, F32),
        shape(256, F32),
        shape(1, F32),
        shape(128, F32),
        shape(1, F32),
    )
    outs = pl.pallas_call(
        last_kernel,
        out_shape=tuple(jax.ShapeDtypeStruct(v.shape, v.dtype) for v in second[:4]) + weights,
        in_specs=[vmem] * 5,
        out_specs=(hbm,) * 12,
        scratch_shapes=[pltpu.VMEM(v.shape, F32) for v in weights] + [pltpu.SemaphoreType.DMA((12,))],
        compiler_params=pltpu.CompilerParams(vmem_limit_bytes=16 * 2**20),
    )(*second)
    return tuple(v.reshape(W) if v.shape[0] == 1 else v for v in outs)


def solution(mesh):
    both = ("stream", "cross")
    rows = P(both, None)
    in_specs = (rows, rows, rows, P(both), P(both), P(both), P(both, None, None), rows, rows) + (P(),) * 8
    out_specs = (rows,) * 4 + (P(),) * 8
    return jax.shard_map(
        per_device, mesh=mesh, in_specs=in_specs, out_specs=out_specs, check_vma=False
    )
```

```python
import math

import jax
import jax.numpy as jnp
from jax import lax
from jax.experimental import pallas as pl
from jax.experimental.pallas import tpu as pltpu
from jax.sharding import PartitionSpec as P

EPSILON = 1e-05
MESH = pl.DeviceIdType.MESH
F32 = jnp.float32
BF16 = jnp.bfloat16
W = 128
NODES = 512
EDGES = 1536
HALO = 128
CHUNK = 1536
TILE = 16
NEAR = 32
FAR = 16
HALF = TILE * NEAR
OWNERS = (32, 25)
PACK = TILE * sum(OWNERS)
ROW_NODE_FIRST = 0
ROW_NODE_SECOND = 256
ROW_EDGE_SECOND = 384
ROW_EDGE_FIRST = 512
ROW_SMALL = 896


def ring_pair(p):
    pair = ((p + 1) // 2) % 4
    turned = ((pair + 1) // 2 + 1) % 2
    return pair, ((p + 1) % 2 + turned) % 2


def ring_place(pair, label):
    turned = ((pair + 1) // 2 + 1) % 2
    return (2 * pair + (label + turned) % 2 + 7) % 8


class Peers:
    def __init__(self, s, c):
        core, x = s % 2, s // 8
        y, z = ((s // 2) % 4) * 2 + c % 2, c // 2
        (wy, ly), (wz, lz) = ring_pair(y), ring_pair(z)
        cores = [core, 1 - core]
        xs = [(x + k) % 4 for k in range(4)]
        self.near_pos = core + 2 * x + 8 * ly + 16 * lz
        self.far_pos = wy + 4 * wz
        ys = [(y, ly), (ring_place(wy, 1 - ly), 1 - ly)]
        zs = [(z, lz), (ring_place(wz, 1 - lz), 1 - lz)]
        near = []
        for kc in range(2):
            for kx in range(4):
                for ky in range(2):
                    for kz in range(2):
                        key = kc + 2 * kx + 8 * ky + 16 * kz
                        hops = (0, 1, 2, 1)[kx] + ky + kz
                        (py, qy), (pz, qz) = ys[ky], zs[kz]
                        at = cores[kc] + 2 * xs[kx] + 8 * qy + 16 * qz
                        near.append((-hops, key, self.device(xs[kx], py, pz, cores[kc]), at))
        far = []
        for ky in range(4):
            for kz in range(4):
                key = ky + 4 * kz
                hops = (0, 2, 3, 2)[ky] + (0, 2, 3, 2)[kz]
                py = ring_place((wy + ky) % 4, ly) if ky else y
                pz = ring_place((wz + kz) % 4, lz) if kz else z
                far.append((-hops, key, self.device(x, py, pz, core)))
        self.near = [p[1:] for p in sorted(near, key=lambda p: p[:2]) if p[1]]
        self.far = [p[1:] for p in sorted(far, key=lambda p: p[:2]) if p[1]]

    @staticmethod
    def device(x, y, z, core):
        return 8 * x + 2 * (y // 2) + core, 2 * z + y % 2


def dot(a, b):
    return jnp.dot(a, b, preferred_element_type=F32)


def dot_nt(a, b):
    return lax.dot_general(a, b, (((1,), (1,)), ((), ())), preferred_element_type=F32)


def dot_tn(a, b):
    return lax.dot_general(a, b, (((0,), (0,)), ((), ())), preferred_element_type=F32)


def columns_of(ref, first, count):
    parts = []
    for k in range(count):
        row = ref[pl.ds(first + k, 1), :]
        parts.append(jnp.broadcast_to(row, (W, W)).T)
    return parts[0] if count == 1 else jnp.concatenate(parts, axis=0)


def hot_rows(col, blocks):
    lane = lax.broadcasted_iota(jnp.int32, col.shape, 1)
    return jnp.concatenate(
        [jnp.where(col == lane + W * j, 1.0, 0.0).astype(BF16) for j in range(blocks)], axis=1
    )


def hot_cols(row, height):
    at = lax.broadcasted_iota(jnp.int32, (height, row.shape[1]), 0)
    return jnp.where(at == row, 1.0, 0.0).astype(BF16)


def sigmoid(v):
    return 0.5 * jnp.tanh(0.5 * v) + 0.5


def normed(z):
    centered = z - jnp.mean(z, axis=-1, keepdims=True)
    rstd = lax.rsqrt(jnp.mean(centered * centered, axis=-1, keepdims=True) + EPSILON)
    return centered * rstd, rstd


def normed_back(dx, xhat, rstd):
    m1 = jnp.mean(dx, axis=-1, keepdims=True)
    m2 = jnp.mean(dx * xhat, axis=-1, keepdims=True)
    return rstd * (dx - m1 - xhat * m2)


def place():
    s = lax.axis_index("stream")
    c = lax.axis_index("cross")
    ns = lax.axis_size("stream")
    nc = lax.axis_size("cross")
    to = [((s + 1, c), s < ns - 1), ((s - 1, c), s > 0), ((s, c + 1), c < nc - 1), ((s, c - 1), c > 0)]
    count = sum(ok.astype(jnp.int32) for _, ok in to)
    return s, c, to, count


BACK = (1, 0, 3, 2)


def first_kernel(
    stale_hbm,
    list_hbm,
    snd_hbm,
    rcv_hbm,
    lat_hbm,
    edge_hbm,
    w1_hbm,
    b1_hbm,
    w2_hbm,
    g_hbm,
    nw1_hbm,
    nb1_hbm,
    nw2_hbm,
    ng_hbm,
    ncot_hbm,
    ecot_hbm,
    count_smem,
    list_ref,
    snd_ref,
    rcv_ref,
    lat_ref,
    edge_ref,
    w1_ref,
    b1_ref,
    w2_ref,
    g_ref,
    nw1_ref,
    nb1_ref,
    nw2_ref,
    ng_ref,
    ncot_ref,
    ecot_ref,
    halo_ref,
    count_ref,
    hot_h_ref,
    hot_r_ref,
    hot_rt_ref,
    rows_s_ref,
    rows_r_ref,
    part_ref,
    stale_ref,
    picked,
    landed,
    load_sem,
    send_sem,
    recv_sem,
):
    s, c, to, count = place()
    barrier = pltpu.get_barrier_semaphore()
    for where, ok in to:

        @pl.when(ok)
        def _(where=where):
            pl.semaphore_signal(barrier, inc=1, device_id=where, device_id_type=MESH)

    pairs = [
        (list_hbm, list_ref),
        (stale_hbm, stale_ref),
        (snd_hbm, snd_ref),
        (rcv_hbm, rcv_ref),
        (lat_hbm, lat_ref),
        (edge_hbm, edge_ref),
        (w1_hbm, w1_ref),
        (b1_hbm, b1_ref),
        (w2_hbm, w2_ref),
        (g_hbm, g_ref),
        (nw1_hbm, nw1_ref),
        (nb1_hbm, nb1_ref),
        (nw2_hbm, nw2_ref),
        (ng_hbm, ng_ref),
        (ncot_hbm, ncot_ref),
        (ecot_hbm, ecot_ref),
    ]
    loads = [pltpu.make_async_copy(a, b, load_sem.at[k]) for k, (a, b) in enumerate(pairs)]
    for load in loads:
        load.start()
    loads[0].wait()
    loads[1].wait()
    table = jnp.concatenate([stale_ref[:256, :], stale_ref[256:, :]], axis=1)
    for k in range(4):
        col = columns_of(list_ref, k, 1)
        both = dot(hot_rows(col & 255, 2), table)
        picked[k] = jnp.where(col < 256, both[:, :W], both[:, W:]).astype(BF16)

    pl.semaphore_wait(barrier, count)

    def copy(k):
        return pltpu.make_async_remote_copy(
            src_ref=picked.at[k],
            dst_ref=landed.at[k],
            send_sem=send_sem.at[k],
            recv_sem=recv_sem.at[k],
            device_id=to[k][0],
            device_id_type=MESH,
        )

    for k in range(4):

        @pl.when(to[k][1])
        def _(k=k):
            copy(k).start()

    for load in loads[2:]:
        load.wait()
    alive_count = count_smem[0]
    count_ref[...] = jnp.full((8, W), alive_count, jnp.int32)
    lat = lat_ref[...]
    per = CHUNK // W
    lane = lax.broadcasted_iota(jnp.int32, (1, W), 1)

    def own_part(i, carry):
        at = pl.ds(i * CHUNK, CHUNK)
        col_s = columns_of(snd_ref, i * per, per)
        col_r = columns_of(rcv_ref, i * per, per)
        row_at = lax.broadcasted_iota(jnp.int32, (CHUNK, W), 0) + i * CHUNK
        hot = hot_rows(jnp.where(row_at < alive_count, col_r, -1), 4)
        hot_r_ref[at, :] = hot
        rows_r = dot(hot, lat).astype(BF16)
        rows_r_ref[at, :] = rows_r
        rows_s = dot(hot_rows(col_s, 4), lat).astype(BF16)
        rows_s_ref[at, :] = rows_s
        hot_h_ref[at, :] = hot_rows(col_s - NODES, 4)
        joined = jnp.concatenate([edge_ref[at, :], rows_s, rows_r], axis=1)
        part_ref[at, :] = dot(joined, w1_ref[...]) + b1_ref[...]
        return carry

    own_part(0, 0)
    for k in range(EDGES // W):
        row = jnp.where(lane + k * W < alive_count, rcv_ref[k : k + 1, :], -1)
        hot_rt_ref[:, k * W : (k + 1) * W] = hot_cols(row, NODES)

    for k in range(4):
        has = to[BACK[k]][1]

        @pl.when(has)
        def _(k=k):
            copy(k).wait_recv()
            halo_ref[HALO * k : HALO * (k + 1), :] = landed[k]

        @pl.when(jnp.logical_not(has))
        def _(k=k):
            halo_ref[HALO * k : HALO * (k + 1), :] = jnp.zeros((HALO, W), BF16)

    for k in range(4):

        @pl.when(to[k][1])
        def _(k=k):
            copy(k).wait_send()


def layer_kernel(
    list_ref,
    snd_ref,
    rcv_ref,
    lat_ref,
    edge_ref,
    w1_ref,
    b1_ref,
    w2_ref,
    g_ref,
    nw1_ref,
    nb1_ref,
    nw2_ref,
    ng_ref,
    ncot_ref,
    ecot_ref,
    halo_ref,
    count_ref,
    hot_h_ref,
    hot_r_ref,
    hot_rt_ref,
    rows_s_ref,
    rows_r_ref,
    part_ref,
    new_ref,
    latg_ref,
    staleg_ref,
    edgeg_ref,
    total,
    rows_s,
    hidden,
    slope,
    xhat_s,
    rstd_s,
    values,
    d_recv,
    d_pre,
    pack,
    near_in,
    near_sum,
    far_in,
    far_sum,
    halo_out,
    halo_in,
    near_send,
    near_recv,
    far_send,
    far_recv,
    all_send,
    all_recv,
    halo_send,
    halo_recv,
):
    s, c, to, count = place()
    peers = Peers(s, c)
    barrier = pltpu.get_barrier_semaphore()
    for peer in peers.near + peers.far:
        pl.semaphore_signal(barrier, inc=1, device_id=peer[1], device_id_type=MESH)
    for where, ok in to:

        @pl.when(ok)
        def _(where=where):
            pl.semaphore_signal(barrier, inc=1, device_id=where, device_id_type=MESH)

    lat = lat_ref[...]
    gain = g_ref[...]
    per = CHUNK // W

    def forward(i, carry):
        at = pl.ds(i * CHUNK, CHUNK)
        rows_h = dot(hot_h_ref[at, :], halo_ref[...]).astype(BF16)
        rows_s[at, :] = rows_s_ref[at, :] + rows_h
        pre = part_ref[at, :] + dot(rows_h, w1_ref[W : 2 * W, :])
        gate = sigmoid(pre)
        act = pre * gate
        slope[at, :] = gate + act * (1.0 - gate)
        act = act.astype(BF16)
        hidden[at, :] = act
        xhat, rstd = normed(dot(act, w2_ref[...]))
        xhat_s[at, :] = xhat
        rstd_s[at, :] = jnp.broadcast_to(rstd, xhat.shape)
        values[at, :W] = (edge_ref[at, :].astype(F32) + xhat * gain).astype(BF16)
        return carry

    forward(0, 0)
    agg = dot(hot_rt_ref[...], values[:, :W]).astype(BF16)

    node_in = jnp.concatenate([lat, agg], axis=1)
    pre = dot(node_in, nw1_ref[...]) + nb1_ref[...]
    gate = sigmoid(pre)
    act = pre * gate
    node_slope = gate + act * (1.0 - gate)
    act = act.astype(BF16)
    xhat, rstd = normed(dot(act, nw2_ref[...]))
    ngain = ng_ref[...]
    new_ref[...] = (lat.astype(F32) + xhat * ngain).astype(BF16)
    dy = ncot_ref[...].astype(F32)
    d_ngain = jnp.sum(dy * xhat, axis=0, keepdims=True)
    dz = normed_back(dy * ngain, xhat, rstd).astype(BF16)
    pack[ROW_NODE_SECOND : ROW_NODE_SECOND + 128, :] = dot_tn(act, dz).astype(BF16)
    dp = dot_nt(dz, nw2_ref[...]) * node_slope
    d_nbias = jnp.sum(dp, axis=0, keepdims=True)
    dp = dp.astype(BF16)
    pack[ROW_NODE_FIRST : ROW_NODE_FIRST + 256, :] = dot_tn(node_in, dp).astype(BF16)
    d_in = dot_nt(dp, nw1_ref[...])
    own = dy + d_in[:, :W]
    d_agg = d_in[:, W:].astype(BF16)

    def backward(i, carry):
        d_gain, d_bias = carry
        at = pl.ds(i * CHUNK, CHUNK)
        ct = ecot_ref[at, :].astype(F32) + dot(hot_r_ref[at, :], d_agg)
        row_at = lax.broadcasted_iota(jnp.int32, (CHUNK, W), 0) + i * CHUNK
        dy = jnp.where(row_at < count_ref[0:1, :], ct, 0.0)
        xhat = xhat_s[at, :]
        d_gain = d_gain + jnp.sum(dy * xhat, axis=0, keepdims=True)
        dz = normed_back(dy * gain, xhat, rstd_s[at, :]).astype(BF16)
        dp = dot_nt(dz, w2_ref[...]) * slope[at, :]
        d_bias = d_bias + jnp.sum(dp, axis=0, keepdims=True)
        d_pre[at, :] = dp.astype(BF16)
        xhat_s[at, :] = ct
        values[at, :W] = dz
        return d_gain, d_bias

    zero = jnp.zeros((1, W), F32)
    d_gain, d_bias = backward(0, (zero, zero))
    pack[ROW_EDGE_SECOND : ROW_EDGE_SECOND + 128, :] = dot_tn(hidden[...], values[:, :W]).astype(BF16)

    def owner(half, at):
        return at < OWNERS[half]

    def tile(half, at):
        return pl.ds(pl.multiple_of(half * HALF + at * TILE, TILE), TILE)

    def await_tiles(sem, count):
        tiles = pack.at[pl.ds(0, count * TILE)]
        pltpu.make_async_copy(tiles, tiles, sem).wait()

    def near_start(half):
        for key, where, at in peers.near:

            @pl.when(owner(half, at))
            def _(key=key, where=where, at=at):
                pltpu.make_async_remote_copy(
                    src_ref=pack.at[tile(half, at)],
                    dst_ref=near_in.at[half, key - 1],
                    send_sem=near_send.at[half],
                    recv_sem=near_recv.at[half],
                    device_id=where,
                    device_id_type=MESH,
                ).start()

    def far_start(half):
        @pl.when(owner(half, peers.near_pos))
        def _():
            await_tiles(near_recv.at[half], NEAR - 1)
            acc = pack[tile(half, peers.near_pos), :].astype(F32)
            for k in range(NEAR - 1):
                acc = acc + near_in[half, k].astype(F32)
            near_sum[half] = acc.astype(BF16)
            for key, where in peers.far:
                pltpu.make_async_remote_copy(
                    src_ref=near_sum.at[half],
                    dst_ref=far_in.at[half, peers.far_pos],
                    send_sem=far_send.at[half],
                    recv_sem=far_recv.at[half],
                    device_id=where,
                    device_id_type=MESH,
                ).start()

    def all_start(half):
        @pl.when(owner(half, peers.near_pos))
        def _():
            await_tiles(far_recv.at[half], FAR - 1)
            far_in[half, peers.far_pos] = near_sum[half]
            acc = far_in[half, 0].astype(F32)
            for k in range(1, FAR):
                acc = acc + far_in[half, k].astype(F32)
            far_sum[half] = acc.astype(BF16)
            for key, where, at in peers.near:
                pltpu.make_async_remote_copy(
                    src_ref=far_sum.at[half],
                    dst_ref=total.at[tile(half, peers.near_pos)],
                    send_sem=all_send.at[half],
                    recv_sem=all_recv.at[half],
                    device_id=where,
                    device_id_type=MESH,
                ).start()
            total[tile(half, peers.near_pos), :] = far_sum[half]

    def await_owners(sem, half):
        @pl.when(owner(half, peers.near_pos))
        def _():
            await_tiles(sem, OWNERS[half] - 1)

        if OWNERS[half] < NEAR:

            @pl.when(jnp.logical_not(owner(half, peers.near_pos)))
            def _():
                await_tiles(sem, OWNERS[half])

    def finish(half):
        await_owners(near_send.at[half], half)

        @pl.when(owner(half, peers.near_pos))
        def _():
            await_tiles(far_send.at[half], FAR - 1)
            await_tiles(all_send.at[half], NEAR - 1)

    pl.semaphore_wait(barrier, count + (NEAR - 1) + (FAR - 1))
    near_start(0)
    for k, rows in enumerate((edge_ref, rows_s, rows_r_ref)):
        first = ROW_EDGE_FIRST + W * k
        pack[first : first + W, :] = dot_tn(rows[...], d_pre[...]).astype(BF16)
    pack[ROW_SMALL:, :] = jnp.concatenate(
        [d_bias, d_gain, d_nbias, d_ngain, jnp.zeros((PACK - ROW_SMALL - 4, W), F32)], axis=0
    ).astype(BF16)
    near_start(1)

    def spread(i, carry):
        at = pl.ds(i * CHUNK, CHUNK)
        d_joined = dot_nt(d_pre[at, :], w1_ref[...])
        edgeg_ref[at, :] = (xhat_s[at, :] + d_joined[:, :W]).astype(BF16)
        mine = columns_of(snd_ref, i * per, per) < 512
        d_s = d_joined[:, W : 2 * W]
        values[at, :] = jnp.concatenate(
            [jnp.where(mine, d_s, 0.0).astype(BF16), jnp.where(mine, 0.0, d_s).astype(BF16)], axis=1
        )
        d_recv[at, :] = d_joined[:, 2 * W :].astype(BF16)
        return carry

    spread(0, 0)
    senders = jnp.concatenate([snd_ref[k : k + 1, :] & 511 for k in range(EDGES // W)], axis=1)
    spread_s = dot(hot_cols(senders, 512), values[...])
    for k in range(4):
        halo_out[k] = spread_s[HALO * k : HALO * (k + 1), W:].astype(BF16)

    def back(k):
        return pltpu.make_async_remote_copy(
            src_ref=halo_out.at[k],
            dst_ref=halo_in.at[k],
            send_sem=halo_send.at[k],
            recv_sem=halo_recv.at[k],
            device_id=to[BACK[k]][0],
            device_id_type=MESH,
        )

    for k in range(4):

        @pl.when(to[BACK[k]][1])
        def _(k=k):
            back(k).start()

    spread_r = dot(hot_rt_ref[...], d_recv[...])
    latg_ref[...] = (own + spread_s[:, :W] + spread_r).astype(BF16)

    far_start(0)
    far_start(1)

    for k in range(4):
        has = to[k][1]

        @pl.when(has)
        def _(k=k):
            back(k).wait_recv()

        @pl.when(jnp.logical_not(has))
        def _(k=k):
            halo_in[k] = jnp.zeros((HALO, W), BF16)

    parts = []
    for k in range(4):
        low = columns_of(list_ref, k, 1) < 256
        came = halo_in[k].astype(F32)
        parts.append(
            jnp.concatenate(
                [jnp.where(low, came, 0.0).astype(BF16), jnp.where(low, 0.0, came).astype(BF16)],
                axis=1,
            )
        )
    listed = jnp.concatenate([list_ref[k : k + 1, :] & 255 for k in range(4)], axis=1)
    stale = dot(hot_cols(listed, 256), jnp.concatenate(parts, axis=0))
    staleg_ref[...] = jnp.concatenate([stale[:, :W], stale[:, W:]], axis=0).astype(BF16)

    all_start(0)
    all_start(1)
    for k in range(4):

        @pl.when(to[BACK[k]][1])
        def _(k=k):
            back(k).wait_send()

    await_owners(all_recv.at[0], 0)
    await_owners(all_recv.at[1], 1)
    finish(0)
    finish(1)


def last_kernel(*refs):
    bulk, total = refs[:4], refs[4]
    outs = refs[5:17]
    scaled, sem = refs[17:25], refs[25]
    copies = [pltpu.make_async_copy(bulk[k], outs[k], sem.at[k]) for k in range(4)]
    for copy in copies:
        copy.start()
    sums = total[...].astype(F32)
    entries = ROW_SMALL * W + 4 * W
    squares = jnp.sum(sums * sums)
    factor = jnp.minimum(1.0, math.sqrt(entries) * lax.rsqrt(jnp.full((1, W), squares, F32)))
    rows = (
        (ROW_EDGE_FIRST, 384),
        (ROW_SMALL, 1),
        (ROW_EDGE_SECOND, 128),
        (ROW_SMALL + 1, 1),
        (ROW_NODE_FIRST, 256),
        (ROW_SMALL + 2, 1),
        (ROW_NODE_SECOND, 128),
        (ROW_SMALL + 3, 1),
    )
    for k, (first, height) in enumerate(rows):
        scaled[k][...] = sums[first : first + height, :] * factor
        copy = pltpu.make_async_copy(scaled[k], outs[4 + k], sem.at[4 + k])
        copy.start()
        copies.append(copy)
    for copy in copies:
        copy.wait()


def per_device(
    latents,
    stale_latents,
    edge_latents,
    senders,
    receivers,
    edge_count,
    send_list,
    node_cotangent,
    edge_cotangent,
    edge_first,
    edge_bias,
    edge_second,
    edge_gain,
    node_first,
    node_bias,
    node_second,
    node_gain,
):
    vmem = pl.BlockSpec(memory_space=pltpu.VMEM)
    hbm = pl.BlockSpec(memory_space=pltpu.HBM)

    def row(v):
        return v.reshape(1, W)

    def far_away(v):
        return pltpu.with_memory_space_constraint(v, pltpu.HBM)

    def shape(rows, dtype, width=W):
        return jax.ShapeDtypeStruct((rows, width), dtype)

    fetched = (
        send_list[0],
        senders.reshape(EDGES // W, W),
        receivers.reshape(EDGES // W, W),
        latents,
        edge_latents,
        edge_first,
        row(edge_bias),
        edge_second,
        row(edge_gain),
        node_first,
        row(node_bias),
        node_second,
        row(node_gain),
        node_cotangent,
        edge_cotangent,
    )
    made = (
        shape(4 * HALO, BF16),
        shape(8, jnp.int32),
        shape(EDGES, BF16, 4 * HALO),
        shape(EDGES, BF16, NODES),
        shape(NODES, BF16, EDGES),
        shape(EDGES, BF16),
        shape(EDGES, BF16),
        shape(EDGES, F32),
    )
    first = pl.pallas_call(
        first_kernel,
        out_shape=tuple(jax.ShapeDtypeStruct(v.shape, v.dtype) for v in fetched) + made,
        in_specs=[hbm] * 16 + [pl.BlockSpec(memory_space=pltpu.SMEM)],
        out_specs=(vmem,) * (len(fetched) + len(made)),
        scratch_shapes=[
            pltpu.VMEM((NODES, W), BF16),
            pltpu.VMEM((4, HALO, W), BF16),
            pltpu.VMEM((4, HALO, W), BF16),
            pltpu.SemaphoreType.DMA((16,)),
            pltpu.SemaphoreType.DMA((4,)),
            pltpu.SemaphoreType.DMA((4,)),
        ],
        compiler_params=pltpu.CompilerParams(
            collective_id=0, has_side_effects=True, vmem_limit_bytes=24 * 2**20
        ),
    )(*(far_away(v) for v in (stale_latents, *fetched)), edge_count)

    second = pl.pallas_call(
        layer_kernel,
        out_shape=(
            shape(NODES, BF16),
            shape(NODES, BF16),
            shape(NODES, BF16),
            shape(EDGES, BF16),
            shape(PACK, BF16),
        ),
        in_specs=[vmem] * len(first),
        out_specs=(vmem,) * 5,
        scratch_shapes=[
            pltpu.VMEM((EDGES, W), BF16),
            pltpu.VMEM((EDGES, W), BF16),
            pltpu.VMEM((EDGES, W), F32),
            pltpu.VMEM((EDGES, W), F32),
            pltpu.VMEM((EDGES, W), F32),
            pltpu.VMEM((EDGES, 256), BF16),
            pltpu.VMEM((EDGES, W), BF16),
            pltpu.VMEM((EDGES, W), BF16),
            pltpu.VMEM((PACK, W), BF16),
            pltpu.VMEM((2, NEAR - 1, TILE, W), BF16),
            pltpu.VMEM((2, TILE, W), BF16),
            pltpu.VMEM((2, FAR, TILE, W), BF16),
            pltpu.VMEM((2, TILE, W), BF16),
            pltpu.VMEM((4, HALO, W), BF16),
            pltpu.VMEM((4, HALO, W), BF16),
        ]
        + [pltpu.SemaphoreType.DMA((2,))] * 6
        + [pltpu.SemaphoreType.DMA((4,))] * 2,
        compiler_params=pltpu.CompilerParams(
            collective_id=1, has_side_effects=True, vmem_limit_bytes=32 * 2**20
        ),
    )(*first)

    weights = (
        shape(384, F32),
        shape(1, F32),
        shape(128, F32),
        shape(1, F32),
        shape(256, F32),
        shape(1, F32),
        shape(128, F32),
        shape(1, F32),
    )
    outs = pl.pallas_call(
        last_kernel,
        out_shape=tuple(jax.ShapeDtypeStruct(v.shape, v.dtype) for v in second[:4]) + weights,
        in_specs=[vmem] * 5,
        out_specs=(hbm,) * 12,
        scratch_shapes=[pltpu.VMEM(v.shape, F32) for v in weights] + [pltpu.SemaphoreType.DMA((12,))],
        compiler_params=pltpu.CompilerParams(vmem_limit_bytes=16 * 2**20),
    )(*second)
    return tuple(v.reshape(W) if v.shape[0] == 1 else v for v in outs)


def solution(mesh):
    both = ("stream", "cross")
    rows = P(both, None)
    in_specs = (rows, rows, rows, P(both), P(both), P(both), P(both, None, None), rows, rows) + (P(),) * 8
    out_specs = (rows,) * 4 + (P(),) * 8
    return jax.shard_map(
        per_device, mesh=mesh, in_specs=in_specs, out_specs=out_specs, check_vma=False
    )
```
